32 devices in a mesh: parts: 2 (over x), src: 8 (over z, y), tile: 2 (over core).
Axes of the slice: x: 2, y: 2, z: 4, core: 2. Of those that a mesh axis runs over, the one named last changes fastest.
Arguments:
- mask_values: bfloat16 [2048, 512], P(('parts', 'tile')), parts along dimension 0, may hold values from -1 to 1
- target_image: float32 [2048, 512], P(('parts', 'tile')), parts along dimension 0, may hold values from 0 to 1.5
- jones_pupil: float32 [2, 3, 2, 128, 128], replicated, may hold values from -1.7 to 1.7
- polar_states: float32 [4, 2, 2], replicated, may hold values from -3 to 3
- source_weights: float32 [64], P(('parts', 'src')), parts along dimension 0, may hold values from 0.25 to 4
- pupil_offsets: int32 [64, 2], P(('parts', 'src')), parts along dimension 0, may hold values from 0 to 64
- polar_ids: int32 [64], P(('parts', 'src')), parts along dimension 0, may hold values from 0 to 3
Outputs:
- intensity: float32 [4, 512, 512], P(('parts', 'tile'), 'src'), parts along dimension 0
- mask_grad: float32 [4, 512, 512], P(('parts', 'tile'), 'src'), parts along dimension 0
- source_grad: float32 [64], P(('parts', 'src')), parts along dimension 0
The draws below stay inside these ranges and needn't reach their ends.
There are 2 independent parts, one for each index of `parts`. The reference program is written for one: setup_inputs(seed, part) draws one part's arguments, and reference() takes and returns one part's arrays. A program takes and returns all parts, laid end to end along the dimension named above; an argument that names none is the same for every part. Nothing has to cross between parts.
All inputs are finite; a program needn't handle non-finite values.
Results may differ from the reference program's by a relative error of at most 0.018.
Values may be sent and summed in bfloat16 or wider, within the bound.
A program may use at most 64 MiB of HBM per device.

```python
import math
import jax
import jax.numpy as jnp
from jax import lax

TH = 512
TW = 512
AMB = 64
K = 64
NPOL = 4
KP = 128
NS = 32
ROWS = 1024
N_TILE = 2


def draw_jones_pupil(key, part):
    key_angle, key_rough = jax.random.split(jax.random.fold_in(key, 11))
    angle = jax.random.uniform(key_angle, (3, 2), jnp.float32, -math.pi, math.pi)
    magnitude = 0.7
    rough = jnp.clip(0.3 * jax.random.normal(key_rough, (2, 3, 2, KP, KP), jnp.float32), -1.0, 1.0)
    common = magnitude * jnp.stack([jnp.cos(angle), jnp.sin(angle)], 0)
    return common[:, :, :, None, None] + rough


def draw_target_image(key, part):
    keys = jax.random.split(jax.random.fold_in(key, 23), 4)
    row_cycles = (jax.random.randint(keys[0], (), 1, 3) * max(1, TH // 64)).astype(jnp.float32)
    col_cycles = (jax.random.randint(keys[1], (), 1, 3) * max(1, TW // 64)).astype(jnp.float32)
    phase = jax.random.uniform(keys[2], (), jnp.float32, -math.pi, math.pi)
    row_pos = jnp.arange(ROWS, dtype=jnp.float32)
    col_pos = jnp.arange(TW, dtype=jnp.float32)
    angle = 2.0 * math.pi * (row_cycles * row_pos[:, None] / TH + col_cycles * col_pos[None, :] / TW) + phase
    smooth = jnp.cos(angle)
    amplitude = 0.45
    rough = jax.random.uniform(keys[3], (ROWS, TW), jnp.float32, -0.25, 0.25)
    return 0.75 + amplitude * smooth + rough


def set_ends(values, stream_key, smallest, largest):
    longest = values.shape.index(max(values.shape))
    spots = []
    for shift in (0, 1):
        where = [jax.random.randint(jax.random.fold_in(stream_key, axis), (), 0, length) for axis, length in enumerate(values.shape)]
        where[longest] = (where[longest] + shift) % values.shape[longest]
        spots.append(tuple(where))
    return values.at[spots[0]].set(smallest).at[spots[1]].set(largest)


def block_levels(own_key, shape, cuts, least, largest):
    def one(dim, blocks):
        steps = jax.random.uniform(jax.random.fold_in(jax.random.fold_in(own_key, 6), dim), (blocks,), jnp.float32, least / len(cuts), largest / len(cuts))
        return jnp.repeat(jnp.exp(steps), shape[dim] // blocks).reshape((-1,) + (1,) * (len(shape) - dim - 1))

    level = one(*cuts[0])
    for cut in cuts[1:]:
        level = level * one(*cut)
    return level


def normal_values(key, shape, spread, reach, held_as=jnp.bfloat16):
    return jnp.clip(spread * jax.random.normal(key, shape, jnp.float32), -reach, reach).astype(held_as)


def setup_inputs(seed: int = 0, part: int = 0) -> dict:
    arg_keys = jax.random.split(jax.random.key(seed), 8)
    part_splits = jax.random.split(jax.random.fold_in(arg_keys[7], part), 8)
    mask_values = jnp.clip(jax.random.uniform(part_splits[0], (ROWS, TW), jnp.float32, -1.0, 1.0) * block_levels(part_splits[0], (ROWS, TW), ((0, 2),), -0.4, 0.0), -1.0, 1.0).astype(jnp.bfloat16)
    target_image = draw_target_image(jax.random.fold_in(jax.random.fold_in(arg_keys[7], part), 71), part)
    jones_pupil = draw_jones_pupil(jax.random.fold_in(arg_keys[7], 71), part)
    polar_states = normal_values(arg_keys[3], (NPOL, 2, 2), 0.7, 3.0, jnp.float32)
    source_weights = jnp.clip(jnp.exp(math.log(4.0) - 2.7725887 * jax.random.uniform(part_splits[4], (NS,), jnp.float32) ** block_levels(part_splits[4], (NS,), ((0, 8),), -0.2, 0.2)), 0.25, 4.0)
    pupil_offsets = set_ends(jax.random.randint(part_splits[5], (NS, 2), 0, K + 1), jax.random.fold_in(part_splits[5], 1), 0, K).astype(jnp.int32)
    polar_ids = set_ends(jax.random.randint(part_splits[6], (NS,), 0, NPOL), jax.random.fold_in(part_splits[6], 1), 0, NPOL - 1).astype(jnp.int32)
    return dict(mask_values=mask_values, target_image=target_image, jones_pupil=jones_pupil, polar_states=polar_states, source_weights=source_weights, pupil_offsets=pupil_offsets, polar_ids=polar_ids)


TWO_PI = 2.0 * math.pi
GRAD_SCALE = 32.0

def tables():
    window = TH + 2 * AMB
    orders = jnp.arange(K, dtype=jnp.int32) - K // 2
    columns = jnp.arange(TW, dtype=jnp.int32)
    win_rows = jnp.arange(window, dtype=jnp.int32)
    core_rows = jnp.arange(TH, dtype=jnp.int32) + AMB
    col_angle = TWO_PI * jnp.mod(columns[:, None] * orders[None, :], TW).astype(jnp.float32) / TW
    row_angle = TWO_PI * jnp.mod(orders[:, None] * win_rows[None, :], window).astype(jnp.float32) / window
    core_angle = TWO_PI * jnp.mod(core_rows[:, None] * orders[None, :], window).astype(jnp.float32) / window
    col_fwd = jnp.concatenate([jnp.cos(col_angle), -jnp.sin(col_angle)], 1).astype(jnp.bfloat16)
    row_fwd = jnp.concatenate([jnp.cos(row_angle), jnp.sin(row_angle)], 0).astype(jnp.bfloat16)
    upper_rows = jnp.concatenate([jnp.cos(core_angle), -jnp.sin(core_angle)], 1)
    lower_rows = jnp.concatenate([jnp.sin(core_angle), jnp.cos(core_angle)], 1)
    row_inv = jnp.concatenate([upper_rows, lower_rows], 0).astype(jnp.bfloat16)
    cos_cols = jnp.cos(col_angle).T
    sin_cols = jnp.sin(col_angle).T
    col_inv = jnp.concatenate([jnp.concatenate([cos_cols, sin_cols], 1), jnp.concatenate([-sin_cols, cos_cols], 1)], 0).astype(jnp.bfloat16)
    return (col_fwd, row_fwd, row_inv, col_inv)

def spectrum(extended, col_fwd, row_fwd):
    partial_dft = jnp.dot(extended, col_fwd, preferred_element_type=jnp.float32).astype(jnp.bfloat16)
    product = jnp.dot(row_fwd, partial_dft, preferred_element_type=jnp.float32)
    norm_scale = 1.0 / math.sqrt((TH + 2 * AMB) * TW)
    spectrum_re = norm_scale * (product[:K, :K] + product[K:, K:])
    spectrum_im = norm_scale * (product[:K, K:] - product[K:, :K])
    return (spectrum_re, spectrum_im)

def pupil_of(jones_pupil, polar_states, offset, state_id):
    one_hot = (jnp.arange(NPOL, dtype=jnp.int32) == state_id.astype(jnp.int32)).astype(jnp.float32)
    jones_vec = lax.optimization_barrier(jnp.sum(one_hot[:, None, None] * polar_states, 0))
    zero_index = jnp.zeros((), jnp.int32)
    window = lax.dynamic_slice(jones_pupil, (zero_index, zero_index, zero_index, offset[0].astype(jnp.int32), offset[1].astype(jnp.int32)), (2, 3, 2, K, K))
    vec_re = jones_vec[0][None, :, None, None]
    vec_im = jones_vec[1][None, :, None, None]
    pupil_re = lax.optimization_barrier(jnp.sum(window[0] * vec_re - window[1] * vec_im, 1))
    pupil_im = lax.optimization_barrier(jnp.sum(window[0] * vec_im + window[1] * vec_re, 1))
    return (pupil_re, pupil_im)

def masked_stack(pupil_re, pupil_im, spectrum_re, spectrum_im):
    masked_re = pupil_re * spectrum_re - pupil_im * spectrum_im
    masked_im = pupil_re * spectrum_im + pupil_im * spectrum_re
    return jnp.concatenate([masked_re, masked_im], 1).astype(jnp.bfloat16)

def row_field_of(stacked, row_inv):
    rows_out = jnp.einsum('ak,ckl->cal', row_inv.astype(jnp.float32), stacked.astype(jnp.float32))
    return jnp.concatenate([rows_out[:, :TH], rows_out[:, TH:]], 2).astype(jnp.bfloat16)

def field_of(row_field, col_inv):
    return jnp.einsum('cpk,kq->cpq', row_field.astype(jnp.float32), col_inv.astype(jnp.float32)) / K

def intensity_of(field):
    return lax.optimization_barrier(jnp.sum(field[..., :TW] * field[..., :TW] + field[..., TW:] * field[..., TW:], 0))

def adjoint_terms(field, residual, weight, pupil_re, pupil_im, row_inv, col_inv, source_total):
    coefficient = 2.0 * weight / (source_total * K)
    doubled = jnp.concatenate([residual, residual], 1)
    field_grad = (coefficient * doubled[None] * field).astype(jnp.bfloat16)
    row_grad = jnp.einsum('cpq,kq->cpk', field_grad.astype(jnp.float32), col_inv.astype(jnp.float32)).astype(jnp.bfloat16)
    stacked = jnp.concatenate([row_grad[..., :K], row_grad[..., K:]], 1)
    masked_grad = jnp.einsum('ak,cal->ckl', row_inv.astype(jnp.float32), stacked.astype(jnp.float32))
    grad_re = masked_grad[:, :K]
    grad_im = masked_grad[:, K:]
    spec_re = lax.optimization_barrier(jnp.sum(pupil_re * grad_re + pupil_im * grad_im, 0))
    spec_im = lax.optimization_barrier(jnp.sum(pupil_re * grad_im - pupil_im * grad_re, 0))
    return (spec_re, spec_im)

def window_grad(grad_re, grad_im, row_fwd, col_fwd):
    norm_scale = 1.0 / math.sqrt((TH + 2 * AMB) * TW)
    top_rows = jnp.concatenate([grad_re, grad_im], 1)
    bottom_rows = jnp.concatenate([-grad_im, grad_re], 1)
    grad_prod = norm_scale * jnp.concatenate([top_rows, bottom_rows], 0)
    grad_partial = jnp.dot(row_fwd.astype(jnp.float32).T, grad_prod, precision=lax.Precision.HIGHEST)
    return jnp.dot(grad_partial, col_fwd.astype(jnp.float32).T, precision=lax.Precision.HIGHEST)

def reference(mask_values, target_image, jones_pupil, polar_states, source_weights, pupil_offsets, polar_ids):
    col_fwd, row_fwd, row_inv, col_inv = tables()
    window = TH + 2 * AMB
    tile_count = N_TILE
    source_total = source_weights.shape[0]
    padded = jnp.pad(mask_values, ((AMB, AMB), (0, 0)))
    spectra = [spectrum(padded[tile_index * TH:tile_index * TH + window], col_fwd, row_fwd) for tile_index in range(tile_count)]
    targets = target_image.reshape(tile_count, TH, TW)

    def forward(running, item):
        weight, offset, state_id = item
        pupil_re, pupil_im = pupil_of(jones_pupil, polar_states, offset, state_id)
        updates = []
        for tile_index in range(tile_count):
            stacked = masked_stack(pupil_re, pupil_im, spectra[tile_index][0], spectra[tile_index][1])
            field = field_of(row_field_of(stacked, row_inv), col_inv)
            updates.append(weight / source_total * intensity_of(field))
        return (running + jnp.stack(updates), jnp.zeros((), jnp.float32))
    intensity, unused = lax.scan(forward, jnp.zeros((tile_count, TH, TW), jnp.float32), (source_weights, pupil_offsets, polar_ids))
    residual = intensity - targets

    def backward(running, item):
        weight, offset, state_id = item
        pupil_re, pupil_im = pupil_of(jones_pupil, polar_states, offset, state_id)
        new_re = []
        new_im = []
        terms = []
        for tile_index in range(tile_count):
            stacked = masked_stack(pupil_re, pupil_im, spectra[tile_index][0], spectra[tile_index][1])
            field = field_of(row_field_of(stacked, row_inv), col_inv)
            terms.append(jnp.sum(residual[tile_index] * intensity_of(field)))
            spec_re, spec_im = adjoint_terms(field, residual[tile_index], weight, pupil_re, pupil_im, row_inv, col_inv, source_total)
            new_re.append(running[0][tile_index] + spec_re)
            new_im.append(running[1][tile_index] + spec_im)
        return ((jnp.stack(new_re), jnp.stack(new_im)), jnp.sum(jnp.stack(terms)))
    empty = jnp.zeros((tile_count, K, K), jnp.float32)
    (grad_re, grad_im), weight_terms = lax.scan(backward, (empty, empty), (source_weights, pupil_offsets, polar_ids))
    source_grad = weight_terms / (tile_count * TH * TW)
    grad_rows = jnp.zeros((tile_count * TH + 2 * AMB, TW), jnp.float32)
    for tile_index in range(tile_count):
        grad_rows = grad_rows.at[tile_index * TH:tile_index * TH + window].add(window_grad(grad_re[tile_index], grad_im[tile_index], row_fwd, col_fwd))
    mask_grad = GRAD_SCALE * grad_rows[AMB:AMB + tile_count * TH].reshape(tile_count, TH, TW)
    return (intensity, mask_grad, source_grad)
```

```python
import functools
import math

import jax
import jax.numpy as jnp
import ml_dtypes
import numpy as np
from jax import lax
from jax.experimental import pallas as pl
from jax.experimental.pallas import tpu as pltpu
from jax.sharding import PartitionSpec as P

AMB = 64
K = 64
GRAD_SCALE = 32.0
LANES = 2 * K
ROWS_16 = 16


def split_bf16(table):
    high = table.astype(ml_dtypes.bfloat16)
    low = (table - high.astype(np.float64)).astype(ml_dtypes.bfloat16)
    return high, low


def tables(th, tw):
    window = th + 2 * AMB
    grid = 2 * K
    orders = np.arange(K) - K // 2
    diffs = np.arange(-(K - 1), K)

    def angle(left, right, period):
        return 2.0 * np.pi * np.mod(np.outer(left, right), period) / period

    bf = lambda x: np.ascontiguousarray(x).astype(ml_dtypes.bfloat16)
    col = angle(np.arange(tw), orders, tw)
    col_fwd = np.concatenate([np.cos(col), -np.sin(col)], 1)
    row = angle(orders, np.arange(window), window)
    row_fwd = np.concatenate([np.cos(row), np.sin(row)], 0)
    row_amb = np.stack([row_fwd[:, th + AMB :], row_fwd[:, :AMB]])
    row_back = row_fwd[:, AMB : AMB + th].T
    amb_back = np.zeros((2, th, 2 * K))
    amb_back[0, th - AMB :] = row_fwd[:, :AMB].T
    amb_back[1, :AMB] = row_fwd[:, th + AMB :].T
    small = angle(np.arange(grid), orders, grid)
    cos, sin = np.cos(small), np.sin(small)
    row_inv = np.concatenate(
        [np.concatenate([cos, -sin], 1), np.concatenate([sin, cos], 1)], 0
    )
    col_inv = np.concatenate(
        [np.concatenate([cos.T, sin.T], 1), np.concatenate([-sin.T, cos.T], 1)], 0
    )
    back = col_inv.T
    col_back = np.concatenate([back, back[:, K:], -back[:, :K]], 1)

    def dirichlet(positions):
        turn = positions[:, None] - np.arange(grid)[None, :] / grid
        return np.cos(2.0 * np.pi * turn[:, :, None] * diffs).sum(-1) / grid

    d_row = dirichlet((np.arange(th) + AMB) / window)
    d_col = dirichlet(np.arange(tw) / tw)
    gram = (tw / grid) * (d_row.T @ d_row)
    return dict(
        col_fwd=bf(col_fwd),
        row_fwd=bf(row_fwd[:, AMB : AMB + th]),
        row_amb=bf(row_amb),
        d_col_t=bf(d_col),
        d_row_t=bf(d_row.T),
        col_inv=bf(col_inv / K),
        row_inv=bf(row_inv),
        gram=np.concatenate(split_bf16(gram), 1),
        row_inv_t=bf(row_inv.T),
        col_back=bf(col_back),
        d_col=bf(np.concatenate([d_col.T, d_col.T], 0)),
        col_fwd_t=bf(col_fwd.T),
        d_row=np.concatenate(split_bf16(d_row), 1),
        row_back=bf(row_back),
        amb_back=bf(amb_back),
    )


OWN_ROWS = ("d_row", "row_back", "amb_back")


def dot(a, b):
    return jnp.dot(a, b, preferred_element_type=jnp.float32)


def kernel(names, sizes, *refs):
    n, local, th, tw, share, owners, block_rows, edges, parts_total = sizes
    grid = 2 * K
    count = len(names)
    offsets, ids, weights, polar = refs[:4]
    hbm = dict(zip(names, refs[4 : 4 + count]))
    image_out, grad_out, source_out = refs[4 + count : 7 + count]
    vmem = dict(zip(names, refs[7 + count : 7 + 2 * count]))
    (
        partial, halo, pupil_a, pupil_b, field, power, target_small,
        part, landed, reduced, whole, spec_send, spec_land, edge_land, sums, sums_land,
        load_sem, halo_sem, scatter_send, scatter_recv, gather_send, gather_recv,
        spec_ssem, spec_rsem, edge_ssem, edge_rsem, sums_sem,
    ) = refs[7 + 2 * count :]
    me = lax.axis_index("src")
    tile = lax.axis_index("tile")
    other = 1 - tile

    barrier = pltpu.get_barrier_semaphore()
    for step in range(n):
        peer = lax.rem(me + step, n)
        if step:
            pl.semaphore_signal(barrier, inc=1, device_id={"src": peer, "tile": tile})
        pl.semaphore_signal(barrier, inc=1, device_id={"src": peer, "tile": other})

    own = pl.ds(pl.multiple_of(me * share, share), share)
    loads = {}
    for i, name in enumerate(names):
        source = hbm[name]
        if name == "amb_back":
            source = source.at[tile, own]
        elif name == "row_amb":
            source = source.at[tile]
        elif name in OWN_ROWS:
            source = source.at[own]
        loads[name] = pltpu.make_async_copy(source, vmem[name], load_sem.at[i])
        loads[name].start()

    def table(name):
        loads[name].wait()
        return vmem[name][...]

    partial[...] = dot(table("mask"), table("col_fwd")).astype(jnp.bfloat16)
    pl.semaphore_wait(barrier, 2 * n - 1)
    rim = pl.ds(pl.multiple_of(other * (th - AMB), ROWS_16), AMB)
    halo_copy = pltpu.make_async_remote_copy(
        src_ref=partial.at[rim], dst_ref=halo, send_sem=halo_sem.at[0], recv_sem=halo_sem.at[1],
        device_id={"tile": other},
    )
    halo_copy.start()
    product = dot(table("row_fwd"), partial[...])

    loads["jones"].wait()
    jones = vmem["jones"]
    lane = lax.broadcasted_iota(jnp.int32, (K, LANES), 1)
    left = lane < K
    for s in range(local):
        first, second, state = offsets[s, 0], offsets[s, 1], ids[s]
        low = lax.rem(LANES - second, LANES)
        high = K - second
        vec = [[polar[state, c, i] for i in range(2)] for c in range(2)]
        for j in range(3):
            win = [
                [jones[(c * 3 + j) * 2 + i, pl.ds(first, K), :] for i in range(2)]
                for c in range(2)
            ]
            real = sum(win[0][i] * vec[0][i] - win[1][i] * vec[1][i] for i in range(2))
            imag = sum(win[0][i] * vec[1][i] + win[1][i] * vec[0][i] for i in range(2))
            rows = slice((s * 3 + j) * K, (s * 3 + j + 1) * K)
            for value, kept in ((real, pupil_a), (imag, pupil_b)):
                kept[rows] = jnp.where(
                    left, pltpu.roll(value, low, 1), pltpu.roll(value, high, 1)
                )

    projected = dot(table("target").astype(jnp.bfloat16), table("d_col_t")).astype(jnp.bfloat16)
    target_small[...] = dot(table("d_row_t"), projected)

    halo_copy.wait()
    product = product + dot(table("row_amb"), halo[...])
    sign = jnp.where(left, 1.0, -1.0)
    norm = 1.0 / math.sqrt((th + 2 * AMB) * tw)
    spec = norm * (product[:K] + sign * pltpu.roll(product[K:], K, 1))
    turned = -sign * pltpu.roll(spec, K, 1)

    col_inv = table("col_inv")
    row_inv = table("row_inv")
    total = jnp.zeros((grid, grid), jnp.float32)
    for s in range(local):
        masked = [
            pupil_a[q * K : (q + 1) * K] * spec + pupil_b[q * K : (q + 1) * K] * turned
            for q in range(3 * s, 3 * s + 3)
        ]
        cols = dot(jnp.concatenate(masked, 0).astype(jnp.bfloat16), col_inv).astype(jnp.bfloat16)
        mixed = jnp.concatenate(
            [
                jnp.concatenate([cols[j * K : (j + 1) * K, :grid], cols[j * K : (j + 1) * K, grid:]], 0)
                for j in range(3)
            ],
            1,
        )
        values = dot(row_inv, mixed)
        field[s] = values
        squares = values[:grid] * values[:grid] + values[grid:] * values[grid:]
        power_s = squares[:, :grid] + squares[:, grid : 2 * grid] + squares[:, 2 * grid :]
        power[s] = power_s
        total = total + (weights[s] / parts_total) * power_s
    part[...] = total.astype(jnp.bfloat16)

    def block(index):
        return pl.ds(pl.multiple_of(index * block_rows, block_rows), block_rows)

    def guarded(condition, run):
        if owners == n:
            run()
        else:
            pl.when(condition)(run)

    scatter, gather = {}, {}
    for step in range(1, n):
        peer = lax.rem(me + step, n)
        to = peer if owners == n else jnp.minimum(peer, owners - 1)
        scatter[step] = pltpu.make_async_remote_copy(
            src_ref=part.at[block(to)], dst_ref=landed.at[step],
            send_sem=scatter_send.at[step], recv_sem=scatter_recv.at[step],
            device_id={"src": peer},
        )
        guarded(peer < owners, scatter[step].start)
    mine = me if owners == n else jnp.minimum(me, owners - 1)

    def reduce_own():
        acc = part[block(mine), :].astype(jnp.float32)
        for step in range(1, n):
            scatter[step].wait_recv()
            acc = acc + landed[step].astype(jnp.float32)
        reduced[...] = acc.astype(jnp.bfloat16)
        for step in range(1, n):
            gather[step].start()
        whole[block(mine), :] = reduced[...]

    for step in range(1, n):
        peer = lax.rem(me + step, n)
        gather[step] = pltpu.make_async_remote_copy(
            src_ref=reduced, dst_ref=whole.at[block(mine)],
            send_sem=gather_send.at[step], recv_sem=gather_recv.at[step],
            device_id={"src": peer},
        )
    guarded(me < owners, reduce_own)
    row_inv_t = table("row_inv_t")
    col_back = table("col_back")
    gram = table("gram")
    for step in range(1, n):
        origin = lax.rem(me + n - step, n)
        guarded(origin < owners, gather[step].wait_recv)

    image = whole[...]
    twice = jnp.concatenate([image, image], 0)
    residual = dot(gram, twice) - target_small[...]
    doubled = jnp.concatenate([residual, residual], 0)

    grad = jnp.zeros((K, LANES), jnp.float32)
    scale = 2.0 / (parts_total * K)
    for s in range(local):
        values = field[s]
        scaled = jnp.concatenate(
            [doubled * values[:, j * grid : (j + 1) * grid] for j in range(3)], 1
        ).astype(jnp.bfloat16)
        rows = dot(row_inv_t, scaled).astype(jnp.bfloat16)
        mixed = jnp.concatenate(
            [
                jnp.concatenate(
                    [rows[:K, j * grid : (j + 1) * grid], rows[K:, j * grid : (j + 1) * grid]], 1
                )
                for j in range(3)
            ],
            0,
        )
        both = dot(mixed, col_back)
        own_grad = jnp.zeros((K, LANES), jnp.float32)
        for j in range(3):
            q = 3 * s + j
            rows_q = slice(q * K, (q + 1) * K)
            pair = both[j * K : (j + 1) * K]
            own_grad = own_grad + pupil_a[rows_q] * pair[:, :LANES] + pupil_b[rows_q] * pair[:, LANES:]
        grad = grad + (scale * weights[s]) * own_grad
    spec_send[...] = (norm * grad).astype(jnp.bfloat16)

    spread, rims = {}, []
    for step in range(1, n):
        peer = lax.rem(me + step, n)
        spread[step] = pltpu.make_async_remote_copy(
            src_ref=spec_send, dst_ref=spec_land.at[step],
            send_sem=spec_ssem.at[step], recv_sem=spec_rsem.at[step],
            device_id={"src": peer},
        )
        spread[step].start()
    for e in range(edges):
        rims.append(
            pltpu.make_async_remote_copy(
                src_ref=spec_send, dst_ref=edge_land.at[me],
                send_sem=edge_ssem.at[e], recv_sem=edge_rsem.at[me],
                device_id={"src": e + tile * (n - edges), "tile": other},
            )
        )
        rims[-1].start()
    for s in range(local):
        sums[s : s + 1, :] = jnp.sum(residual * power[s], 0, keepdims=True)
    sums_copy = pltpu.make_async_remote_copy(
        src_ref=sums, dst_ref=sums_land, send_sem=sums_sem.at[0], recv_sem=sums_sem.at[1],
        device_id={"tile": other},
    )
    sums_copy.start()

    lines = dot(table("d_row"), twice)
    lines_high = lines.astype(jnp.bfloat16)
    lines_low = (lines - lines_high.astype(jnp.float32)).astype(jnp.bfloat16)
    image_out[0] = dot(jnp.concatenate([lines_high, lines_low], 1), table("d_col"))

    row_back, amb_back, col_fwd_t = table("row_back"), table("amb_back"), table("col_fwd_t")
    sums_copy.wait()
    both_sums = sums[...] + sums_land[...]
    for s in range(local):
        source_out[s] = jnp.sum(both_sums[s : s + 1, :]) / (2 * th * tw)

    def stack(value):
        return jnp.concatenate([value, -sign * pltpu.roll(value, K, 1)], 0).astype(jnp.bfloat16)

    summed = spec_send[...].astype(jnp.float32)
    for step in range(1, n):
        spread[step].wait_recv()
        summed = summed + spec_land[step].astype(jnp.float32)
    rows = dot(row_back, stack(summed))
    at_rim = jnp.where(tile == 0, me >= n - edges, me < edges)

    @pl.when(at_rim)
    def _():
        outer = jnp.zeros((K, LANES), jnp.float32)
        for d in range(n):
            pltpu.make_async_remote_copy(
                src_ref=spec_send, dst_ref=edge_land.at[d],
                send_sem=edge_ssem.at[0], recv_sem=edge_rsem.at[d],
                device_id={"tile": other},
            ).wait_recv()
            outer = outer + edge_land[d].astype(jnp.float32)
        full = rows + dot(amb_back, stack(outer))
        grad_out[0] = GRAD_SCALE * dot(full.astype(jnp.bfloat16), col_fwd_t)

    @pl.when(jnp.logical_not(at_rim))
    def _():
        grad_out[0] = GRAD_SCALE * dot(rows.astype(jnp.bfloat16), col_fwd_t)

    for step in range(1, n):
        guarded(lax.rem(me + step, n) < owners, scatter[step].wait_send)
        guarded(me < owners, gather[step].wait_send)
        spread[step].wait_send()
    for copy in rims:
        copy.wait_send()


def body(
    mask_values, target_image, jones_pupil, polar_states, source_weights, pupil_offsets, polar_ids
):
    th, tw = mask_values.shape
    n = lax.axis_size("src")
    assert lax.axis_size("tile") == 2
    local = source_weights.shape[0]
    share = th // n
    grid = 2 * K
    owners = min(n, grid // ROWS_16)
    block_rows = grid // owners
    assert owners * block_rows == grid
    edges = -(-AMB // share)
    named = dict(
        mask=mask_values,
        target=target_image,
        jones=jones_pupil.reshape((-1,) + jones_pupil.shape[-2:]),
    )
    constants = tables(th, tw)
    order = ["mask", "col_fwd", "row_fwd", "jones", "target", "d_col_t", "d_row_t"]
    order += [name for name in constants if name not in order]
    arrays = []
    held = []
    for name in order:
        value = named[name] if name in named else jnp.asarray(constants[name])
        arrays.append(value)
        shape = value.shape
        if name == "amb_back":
            shape = (share,) + shape[2:]
        elif name == "row_amb":
            shape = shape[1:]
        elif name in OWN_ROWS:
            shape = (share,) + shape[1:]
        held.append(pltpu.VMEM(shape, value.dtype))
    f32, bf16 = jnp.float32, jnp.bfloat16
    sems = pltpu.SemaphoreType.DMA
    scratch = held + [
        pltpu.VMEM((th, LANES), bf16),
        pltpu.VMEM((AMB, LANES), bf16),
        pltpu.VMEM((3 * local * K, LANES), f32),
        pltpu.VMEM((3 * local * K, LANES), f32),
        pltpu.VMEM((local, 2 * grid, 3 * grid), f32),
        pltpu.VMEM((local, grid, grid), f32),
        pltpu.VMEM((grid, grid), f32),
        pltpu.VMEM((grid, grid), bf16),
        pltpu.VMEM((n, block_rows, grid), bf16),
        pltpu.VMEM((block_rows, grid), bf16),
        pltpu.VMEM((grid, grid), bf16),
        pltpu.VMEM((K, LANES), bf16),
        pltpu.VMEM((n, K, LANES), bf16),
        pltpu.VMEM((n, K, LANES), bf16),
        pltpu.VMEM((local, LANES), f32),
        pltpu.VMEM((local, LANES), f32),
        sems((len(order),)),
        sems((2,)),
        sems((n,)),
        sems((n,)),
        sems((n,)),
        sems((n,)),
        sems((n,)),
        sems((n,)),
        sems((edges,)),
        sems((n,)),
        sems((2,)),
    ]
    sizes = (n, local, th, tw, share, owners, block_rows, edges, local * n)
    smem = pl.BlockSpec(memory_space=pltpu.SMEM)
    return pl.pallas_call(
        functools.partial(kernel, tuple(order), sizes),
        out_shape=(
            jax.ShapeDtypeStruct((1, share, tw), f32),
            jax.ShapeDtypeStruct((1, share, tw), f32),
            jax.ShapeDtypeStruct((local,), f32),
        ),
        in_specs=[smem] * 4 + [pl.BlockSpec(memory_space=pl.ANY)] * len(arrays),
        out_specs=(
            pl.BlockSpec(memory_space=pltpu.VMEM),
            pl.BlockSpec(memory_space=pltpu.VMEM),
            smem,
        ),
        scratch_shapes=scratch,
        compiler_params=pltpu.CompilerParams(
            collective_id=0, has_side_effects=True, vmem_limit_bytes=48 * 1024 * 1024
        ),
    )(pupil_offsets, polar_ids, source_weights, polar_states, *arrays)


def solution(mesh):
    placed = (
        P(("parts", "tile"), None),
        P(("parts", "tile"), None),
        P(),
        P(),
        P(("parts", "src")),
        P(("parts", "src"), None),
        P(("parts", "src")),
    )
    return jax.shard_map(
        body,
        mesh=mesh,
        in_specs=placed,
        out_specs=(
            P(("parts", "tile"), "src", None),
            P(("parts", "tile"), "src", None),
            P(("parts", "src")),
        ),
        check_vma=False,
    )
```

```python
import functools
import math

import jax
import jax.numpy as jnp
import ml_dtypes
import numpy as np
from jax import lax
from jax.experimental import pallas as pl
from jax.experimental.pallas import tpu as pltpu
from jax.sharding import PartitionSpec as P

AMB = 64
K = 64
GRAD_SCALE = 32.0
LANES = 2 * K
VMEM_LIMIT = 64 * 1024 * 1024 - 512 * 1024
ROWS_16 = 16


def split_bf16(table):
    high = table.astype(ml_dtypes.bfloat16)
    low = (table - high.astype(np.float64)).astype(ml_dtypes.bfloat16)
    return high, low


def tables(th, tw):
    window = th + 2 * AMB
    grid = 2 * K
    orders = np.arange(K) - K // 2
    diffs = np.arange(-(K - 1), K)

    def angle(left, right, period):
        return 2.0 * np.pi * np.mod(np.outer(left, right), period) / period

    bf = lambda x: np.ascontiguousarray(x).astype(ml_dtypes.bfloat16)
    col = angle(np.arange(tw), orders, tw)
    col_fwd = np.concatenate([np.cos(col), -np.sin(col)], 1)
    row = angle(orders, np.arange(window), window)
    row_fwd = np.concatenate([np.cos(row), np.sin(row)], 0)
    row_amb = np.stack([row_fwd[:, th + AMB :], row_fwd[:, :AMB]])
    row_back = row_fwd[:, AMB : AMB + th].T
    amb_back = np.zeros((2, th, 2 * K))
    amb_back[0, th - AMB :] = row_fwd[:, :AMB].T
    amb_back[1, :AMB] = row_fwd[:, th + AMB :].T
    small = angle(np.arange(grid), orders, grid)
    cos, sin = np.cos(small), np.sin(small)
    row_inv = np.concatenate(
        [np.concatenate([cos, -sin], 1), np.concatenate([sin, cos], 1)], 0
    )
    col_inv = np.concatenate(
        [np.concatenate([cos.T, sin.T], 1), np.concatenate([-sin.T, cos.T], 1)], 0
    )
    back = col_inv.T
    col_back = np.concatenate([back, back[:, K:], -back[:, :K]], 1)

    def dirichlet(positions):
        turn = positions[:, None] - np.arange(grid)[None, :] / grid
        return np.cos(2.0 * np.pi * turn[:, :, None] * diffs).sum(-1) / grid

    d_row = dirichlet((np.arange(th) + AMB) / window)
    d_col = dirichlet(np.arange(tw) / tw)
    gram = (tw / grid) * (d_row.T @ d_row)
    return dict(
        col_fwd=bf(col_fwd),
        row_fwd=bf(row_fwd[:, AMB : AMB + th]),
        row_amb=bf(row_amb),
        d_col_t=bf(d_col),
        d_row_t=bf(d_row.T),
        col_inv=bf(col_inv / K),
        row_inv=bf(row_inv),
        gram=np.concatenate(split_bf16(gram), 1),
        row_inv_t=bf(row_inv.T),
        col_back=bf(col_back),
        d_col=bf(np.concatenate([d_col.T, d_col.T], 0)),
        col_fwd_t=bf(col_fwd.T),
        d_row=np.concatenate(split_bf16(d_row), 1),
        row_back=bf(row_back),
        amb_back=bf(amb_back),
    )


SCALARS = ("offsets", "ids", "weights", "polar")
OWN_ROWS = ("d_row", "row_back", "amb_back")


def dot(a, b):
    return jnp.dot(a, b, preferred_element_type=jnp.float32)


def kernel(names, sizes, *refs):
    n, local, th, tw, share, owners, block_rows, edges, parts_total = sizes
    grid = 2 * K
    count = len(names)
    hbm = dict(zip(names, refs[:count]))
    outputs = refs[count : 3 + count]
    vmem = dict(zip(names, refs[3 + count : 3 + 2 * count]))
    offsets, ids, weights, polar = (vmem[name] for name in SCALARS)
    (
        partial, halo, pupil_a, pupil_b, field, power, target_small,
        part, landed, reduced, whole, spec_send, spec_land, edge_land, sums, sums_land,
        load_sem, halo_sem, scatter_send, scatter_recv, gather_send, gather_recv,
        spec_ssem, spec_rsem, edge_ssem, edge_rsem, sums_sem,
        image_out, grad_out, source_out, out_sem,
    ) = refs[3 + 2 * count :]
    me = lax.axis_index("src")
    tile = lax.axis_index("tile")
    other = 1 - tile

    barrier = pltpu.get_barrier_semaphore()
    for step in range(n):
        peer = lax.rem(me + step, n)
        if step:
            pl.semaphore_signal(barrier, inc=1, device_id={"src": peer, "tile": tile})
        pl.semaphore_signal(barrier, inc=1, device_id={"src": peer, "tile": other})

    own = pl.ds(pl.multiple_of(me * share, share), share)
    loads = {}
    for i, name in enumerate(names):
        source = hbm[name]
        if name == "amb_back":
            source = source.at[tile, own]
        elif name == "row_amb":
            source = source.at[tile]
        elif name in OWN_ROWS:
            source = source.at[own]
        loads[name] = pltpu.make_async_copy(source, vmem[name], load_sem.at[i])
        loads[name].start()

    def table(name):
        loads[name].wait()
        return vmem[name][...]

    partial[...] = dot(table("mask"), table("col_fwd")).astype(jnp.bfloat16)
    for name in SCALARS + ("jones",):
        loads[name].wait()
    jones = vmem["jones"]
    lane = lax.broadcasted_iota(jnp.int32, (K, LANES), 1)
    left = lane < K
    for s in range(local):
        first, second, state = offsets[0, s], offsets[1, s], ids[s]
        low = lax.rem(LANES - second, LANES)
        high = K - second
        vec = [[polar[c, i, state] for i in range(2)] for c in range(2)]
        for j in range(3):
            win = [
                [jones[(c * 3 + j) * 2 + i, pl.ds(first, K), :] for i in range(2)]
                for c in range(2)
            ]
            real = sum(win[0][i] * vec[0][i] - win[1][i] * vec[1][i] for i in range(2))
            imag = sum(win[0][i] * vec[1][i] + win[1][i] * vec[0][i] for i in range(2))
            rows = slice((s * 3 + j) * K, (s * 3 + j + 1) * K)
            for value, kept in ((real, pupil_a), (imag, pupil_b)):
                kept[rows] = jnp.where(
                    left, pltpu.roll(value, low, 1), pltpu.roll(value, high, 1)
                )

    pl.semaphore_wait(barrier, 2 * n - 1)
    rim = pl.ds(pl.multiple_of(other * (th - AMB), ROWS_16), AMB)
    halo_copy = pltpu.make_async_remote_copy(
        src_ref=partial.at[rim], dst_ref=halo, send_sem=halo_sem.at[0], recv_sem=halo_sem.at[1],
        device_id={"tile": other},
    )
    halo_copy.start()
    product = dot(table("row_fwd"), partial[...])

    projected = dot(table("target").astype(jnp.bfloat16), table("d_col_t")).astype(jnp.bfloat16)
    target_small[...] = dot(table("d_row_t"), projected)

    halo_copy.wait()
    product = product + dot(table("row_amb"), halo[...])
    sign = jnp.where(left, 1.0, -1.0)
    norm = 1.0 / math.sqrt((th + 2 * AMB) * tw)
    spec = norm * (product[:K] + sign * pltpu.roll(product[K:], K, 1))
    turned = -sign * pltpu.roll(spec, K, 1)

    col_inv = table("col_inv")
    row_inv = table("row_inv")
    total = jnp.zeros((grid, grid), jnp.float32)
    for s in range(local):
        masked = [
            pupil_a[q * K : (q + 1) * K] * spec + pupil_b[q * K : (q + 1) * K] * turned
            for q in range(3 * s, 3 * s + 3)
        ]
        cols = dot(jnp.concatenate(masked, 0).astype(jnp.bfloat16), col_inv).astype(jnp.bfloat16)
        mixed = jnp.concatenate(
            [
                jnp.concatenate([cols[j * K : (j + 1) * K, :grid], cols[j * K : (j + 1) * K, grid:]], 0)
                for j in range(3)
            ],
            1,
        )
        values = dot(row_inv, mixed)
        field[s] = values
        squares = values[:grid] * values[:grid] + values[grid:] * values[grid:]
        power_s = squares[:, :grid] + squares[:, grid : 2 * grid] + squares[:, 2 * grid :]
        power[s] = power_s
        total = total + (weights[s] / parts_total) * power_s
    part[...] = total.astype(jnp.bfloat16)

    def block(index):
        return pl.ds(pl.multiple_of(index * block_rows, block_rows), block_rows)

    def guarded(condition, run):
        if owners == n:
            run()
        else:
            pl.when(condition)(run)

    scatter, gather = {}, {}
    for step in range(1, n):
        peer = lax.rem(me + step, n)
        to = peer if owners == n else jnp.minimum(peer, owners - 1)
        scatter[step] = pltpu.make_async_remote_copy(
            src_ref=part.at[block(to)], dst_ref=landed.at[step],
            send_sem=scatter_send.at[step], recv_sem=scatter_recv.at[step],
            device_id={"src": peer},
        )
        guarded(peer < owners, scatter[step].start)
    mine = me if owners == n else jnp.minimum(me, owners - 1)

    def reduce_own():
        acc = part[block(mine), :].astype(jnp.float32)
        for step in range(1, n):
            scatter[step].wait_recv()
            acc = acc + landed[step].astype(jnp.float32)
        reduced[...] = acc.astype(jnp.bfloat16)
        for step in range(1, n):
            gather[step].start()
        whole[block(mine), :] = reduced[...]

    for step in range(1, n):
        peer = lax.rem(me + step, n)
        gather[step] = pltpu.make_async_remote_copy(
            src_ref=reduced, dst_ref=whole.at[block(mine)],
            send_sem=gather_send.at[step], recv_sem=gather_recv.at[step],
            device_id={"src": peer},
        )
    guarded(me < owners, reduce_own)
    row_inv_t = table("row_inv_t")
    col_back = table("col_back")
    gram = table("gram")
    for step in range(1, n):
        origin = lax.rem(me + n - step, n)
        guarded(origin < owners, gather[step].wait_recv)

    image = whole[...]
    twice = jnp.concatenate([image, image], 0)
    residual = dot(gram, twice) - target_small[...]
    doubled = jnp.concatenate([residual, residual], 0)

    grad = jnp.zeros((K, LANES), jnp.float32)
    scale = 2.0 / (parts_total * K)
    for s in range(local):
        values = field[s]
        scaled = jnp.concatenate(
            [doubled * values[:, j * grid : (j + 1) * grid] for j in range(3)], 1
        ).astype(jnp.bfloat16)
        rows = dot(row_inv_t, scaled).astype(jnp.bfloat16)
        mixed = jnp.concatenate(
            [
                jnp.concatenate(
                    [rows[:K, j * grid : (j + 1) * grid], rows[K:, j * grid : (j + 1) * grid]], 1
                )
                for j in range(3)
            ],
            0,
        )
        both = dot(mixed, col_back)
        own_grad = jnp.zeros((K, LANES), jnp.float32)
        for j in range(3):
            q = 3 * s + j
            rows_q = slice(q * K, (q + 1) * K)
            pair = both[j * K : (j + 1) * K]
            own_grad = own_grad + pupil_a[rows_q] * pair[:, :LANES] + pupil_b[rows_q] * pair[:, LANES:]
        grad = grad + (scale * weights[s]) * own_grad
    spec_send[...] = (norm * grad).astype(jnp.bfloat16)

    spread, rims = {}, []
    for step in range(1, n):
        peer = lax.rem(me + step, n)
        spread[step] = pltpu.make_async_remote_copy(
            src_ref=spec_send, dst_ref=spec_land.at[step],
            send_sem=spec_ssem.at[step], recv_sem=spec_rsem.at[step],
            device_id={"src": peer},
        )
        spread[step].start()
    for e in range(edges):
        rims.append(
            pltpu.make_async_remote_copy(
                src_ref=spec_send, dst_ref=edge_land.at[me],
                send_sem=edge_ssem.at[e], recv_sem=edge_rsem.at[me],
                device_id={"src": e + tile * (n - edges), "tile": other},
            )
        )
        rims[-1].start()
    for s in range(local):
        sums[s : s + 1, :] = jnp.sum(residual * power[s], 0, keepdims=True)
    sums_copy = pltpu.make_async_remote_copy(
        src_ref=sums, dst_ref=sums_land, send_sem=sums_sem.at[0], recv_sem=sums_sem.at[1],
        device_id={"tile": other},
    )
    sums_copy.start()

    lines = dot(table("d_row"), twice)
    lines_high = lines.astype(jnp.bfloat16)
    lines_low = (lines - lines_high.astype(jnp.float32)).astype(jnp.bfloat16)
    image_out[...] = dot(jnp.concatenate([lines_high, lines_low], 1), table("d_col"))

    writes = [
        pltpu.make_async_copy(source, to, out_sem.at[i])
        for i, (source, to) in enumerate(zip((image_out, grad_out, source_out), outputs))
    ]
    writes[0].start()

    row_back, amb_back, col_fwd_t = table("row_back"), table("amb_back"), table("col_fwd_t")
    sums_copy.wait()
    both_sums = jnp.sum(sums[...] + sums_land[...], 1, keepdims=True) / (2 * th * tw)
    for s in range(local):
        source_out[s] = both_sums[s, 0]
    writes[2].start()

    def stack(value):
        return jnp.concatenate([value, -sign * pltpu.roll(value, K, 1)], 0).astype(jnp.bfloat16)

    summed = spec_send[...].astype(jnp.float32)
    for step in range(1, n):
        spread[step].wait_recv()
        summed = summed + spec_land[step].astype(jnp.float32)
    rows = dot(row_back, stack(summed))
    at_rim = jnp.where(tile == 0, me >= n - edges, me < edges)

    @pl.when(at_rim)
    def _():
        outer = jnp.zeros((K, LANES), jnp.float32)
        for d in range(n):
            pltpu.make_async_remote_copy(
                src_ref=spec_send, dst_ref=edge_land.at[d],
                send_sem=edge_ssem.at[0], recv_sem=edge_rsem.at[d],
                device_id={"tile": other},
            ).wait_recv()
            outer = outer + edge_land[d].astype(jnp.float32)
        full = rows + dot(amb_back, stack(outer))
        grad_out[...] = GRAD_SCALE * dot(full.astype(jnp.bfloat16), col_fwd_t)

    @pl.when(jnp.logical_not(at_rim))
    def _():
        grad_out[...] = GRAD_SCALE * dot(rows.astype(jnp.bfloat16), col_fwd_t)

    writes[1].start()
    for step in range(1, n):
        guarded(lax.rem(me + step, n) < owners, scatter[step].wait_send)
        guarded(me < owners, gather[step].wait_send)
        spread[step].wait_send()
    for copy in rims:
        copy.wait_send()
    for copy in writes:
        copy.wait()


def write_outputs(image, grad, source, image_out, grad_out, source_out, sem):
    copies = [
        pltpu.make_async_copy(image, image_out.at[0], sem.at[0]),
        pltpu.make_async_copy(grad, grad_out.at[0], sem.at[1]),
        pltpu.make_async_copy(source, source_out, sem.at[2]),
    ]
    for copy in copies:
        copy.start()
    for copy in copies:
        copy.wait()


def body(
    mask_values, target_image, jones_pupil, polar_states, source_weights, pupil_offsets, polar_ids
):
    th, tw = mask_values.shape
    n = lax.axis_size("src")
    assert lax.axis_size("tile") == 2
    local = source_weights.shape[0]
    share = th // n
    grid = 2 * K
    owners = min(n, grid // ROWS_16)
    block_rows = grid // owners
    assert owners * block_rows == grid
    edges = -(-AMB // share)
    named = dict(
        mask=mask_values,
        target=target_image,
        jones=jones_pupil.reshape((-1,) + jones_pupil.shape[-2:]),
        offsets=pupil_offsets.T,
        ids=polar_ids,
        weights=source_weights,
        polar=polar_states.transpose(1, 2, 0),
    )
    constants = tables(th, tw)
    order = ["mask", "col_fwd", *SCALARS, "jones", "row_fwd", "target", "d_col_t", "d_row_t"]
    order += [name for name in constants if name not in order]
    arrays = []
    held = []
    for name in order:
        value = named[name] if name in named else jnp.asarray(constants[name])
        arrays.append(value)
        shape = value.shape
        if name == "amb_back":
            shape = (share,) + shape[2:]
        elif name == "row_amb":
            shape = shape[1:]
        elif name in OWN_ROWS:
            shape = (share,) + shape[1:]
        held.append((pltpu.SMEM if name in SCALARS else pltpu.VMEM)(shape, value.dtype))
    f32, bf16 = jnp.float32, jnp.bfloat16
    sems = pltpu.SemaphoreType.DMA
    scratch = held + [
        pltpu.VMEM((th, LANES), bf16),
        pltpu.VMEM((AMB, LANES), bf16),
        pltpu.VMEM((3 * local * K, LANES), f32),
        pltpu.VMEM((3 * local * K, LANES), f32),
        pltpu.VMEM((local, 2 * grid, 3 * grid), f32),
        pltpu.VMEM((local, grid, grid), f32),
        pltpu.VMEM((grid, grid), f32),
        pltpu.VMEM((grid, grid), bf16),
        pltpu.VMEM((n, block_rows, grid), bf16),
        pltpu.VMEM((block_rows, grid), bf16),
        pltpu.VMEM((grid, grid), bf16),
        pltpu.VMEM((K, LANES), bf16),
        pltpu.VMEM((n, K, LANES), bf16),
        pltpu.VMEM((n, K, LANES), bf16),
        pltpu.VMEM((local, LANES), f32),
        pltpu.VMEM((local, LANES), f32),
        sems((len(order),)),
        sems((2,)),
        sems((n,)),
        sems((n,)),
        sems((n,)),
        sems((n,)),
        sems((n,)),
        sems((n,)),
        sems((edges,)),
        sems((n,)),
        sems((2,)),
        pltpu.VMEM((share, tw), f32),
        pltpu.VMEM((share, tw), f32),
        pltpu.SMEM((local,), f32),
        sems((3,)),
    ]
    sizes = (n, local, th, tw, share, owners, block_rows, edges, local * n)
    in_hbm = pl.BlockSpec(memory_space=pltpu.HBM)
    results = pl.pallas_call(
        functools.partial(kernel, tuple(order), sizes),
        out_shape=(
            jax.ShapeDtypeStruct((share, tw), f32),
            jax.ShapeDtypeStruct((share, tw), f32),
            jax.ShapeDtypeStruct((local,), f32),
        ),
        in_specs=[in_hbm] * len(arrays),
        out_specs=(in_hbm,) * 3,
        scratch_shapes=scratch,
        compiler_params=pltpu.CompilerParams(
            collective_id=0, has_side_effects=True, vmem_limit_bytes=VMEM_LIMIT
        ),
    )(*arrays)
    return pl.pallas_call(
        write_outputs,
        out_shape=(
            jax.ShapeDtypeStruct((1, share, tw), f32),
            jax.ShapeDtypeStruct((1, share, tw), f32),
            jax.ShapeDtypeStruct((local,), f32),
        ),
        in_specs=[in_hbm] * 3,
        out_specs=(in_hbm,) * 3,
        scratch_shapes=[sems((3,))],
        compiler_params=pltpu.CompilerParams(vmem_limit_bytes=VMEM_LIMIT),
    )(*results)


def solution(mesh):
    placed = (
        P(("parts", "tile"), None),
        P(("parts", "tile"), None),
        P(),
        P(),
        P(("parts", "src")),
        P(("parts", "src"), None),
        P(("parts", "src")),
    )
    return jax.shard_map(
        body,
        mesh=mesh,
        in_specs=placed,
        out_specs=(
            P(("parts", "tile"), "src", None),
            P(("parts", "tile"), "src", None),
            P(("parts", "src")),
        ),
        check_vma=False,
    )
```

```python
import functools
import math

import jax
import jax.numpy as jnp
import ml_dtypes
import numpy as np
from jax import lax
from jax.experimental import pallas as pl
from jax.experimental.pallas import tpu as pltpu
from jax.sharding import PartitionSpec as P

AMB = 64
K = 64
GRAD_SCALE = 32.0
LANES = 2 * K
VMEM_LIMIT = 64 * 1024 * 1024 - 512 * 1024
ROWS_16 = 16


def split_bf16(table):
    high = table.astype(ml_dtypes.bfloat16)
    low = (table - high.astype(np.float64)).astype(ml_dtypes.bfloat16)
    return high, low


def tables(th, tw):
    window = th + 2 * AMB
    grid = 2 * K
    orders = np.arange(K) - K // 2
    diffs = np.arange(-(K - 1), K)

    def angle(left, right, period):
        return 2.0 * np.pi * np.mod(np.outer(left, right), period) / period

    bf = lambda x: np.ascontiguousarray(x).astype(ml_dtypes.bfloat16)
    col = angle(np.arange(tw), orders, tw)
    col_fwd = np.concatenate([np.cos(col), -np.sin(col)], 1)
    row = angle(orders, np.arange(window), window)
    row_fwd = np.concatenate([np.cos(row), np.sin(row)], 0)
    row_amb = np.stack([row_fwd[:, th + AMB :], row_fwd[:, :AMB]])
    row_back = row_fwd[:, AMB : AMB + th].T
    amb_back = np.zeros((2, th, 2 * K))
    amb_back[0, th - AMB :] = row_fwd[:, :AMB].T
    amb_back[1, :AMB] = row_fwd[:, th + AMB :].T
    small = angle(np.arange(grid), orders, grid)
    cos, sin = np.cos(small), np.sin(small)
    row_inv = np.concatenate(
        [np.concatenate([cos, -sin], 1), np.concatenate([sin, cos], 1)], 0
    )
    col_inv = np.concatenate(
        [np.concatenate([cos.T, sin.T], 1), np.concatenate([-sin.T, cos.T], 1)], 0
    )
    back = col_inv.T
    col_back = np.concatenate([back, back[:, K:], -back[:, :K]], 1)

    def dirichlet(positions):
        turn = positions[:, None] - np.arange(grid)[None, :] / grid
        return np.cos(2.0 * np.pi * turn[:, :, None] * diffs).sum(-1) / grid

    d_row = dirichlet((np.arange(th) + AMB) / window)
    d_col = dirichlet(np.arange(tw) / tw)
    gram = (tw / grid) * (d_row.T @ d_row)
    return dict(
        col_fwd=bf(col_fwd),
        row_fwd=bf(row_fwd[:, AMB : AMB + th]),
        row_amb=bf(row_amb),
        d_col_t=bf(d_col),
        d_row_t=bf(d_row.T),
        col_inv=bf(col_inv / K),
        row_inv=bf(row_inv),
        gram=np.concatenate(split_bf16(gram), 1),
        row_inv_t=bf(row_inv.T),
        col_back=bf(col_back),
        d_col=bf(np.concatenate([d_col.T, d_col.T], 0)),
        col_fwd_t=bf(col_fwd.T),
        d_row=np.concatenate(split_bf16(d_row), 1),
        row_back=bf(row_back),
        amb_back=bf(amb_back),
    )


SCALARS = ("offsets", "ids", "weights", "polar")
FIRST = ("mask", "col_fwd")
SECOND = SCALARS + ("jones", "row_fwd", "row_amb", "col_inv", "row_inv")
OWN_ROWS = ("d_row", "row_back", "amb_back")


def dot(a, b):
    return jnp.dot(a, b, preferred_element_type=jnp.float32)


def kernel(names, sizes, *refs):
    n, local, th, tw, share, owners, block_rows, edges, parts_total = sizes
    grid = 2 * K
    count = len(names)
    hbm = dict(zip(names, refs[:count]))
    outputs = refs[count : 3 + count]
    vmem = dict(zip(names, refs[3 + count : 3 + 2 * count]))
    offsets, ids, weights, polar = (vmem[name] for name in SCALARS)
    (
        partial, halo, pupil_a, pupil_b, field, power, target_small,
        part, landed, reduced, whole, spec_send, spec_land, edge_land, sums, sums_land,
        load_sem, halo_sem, scatter_send, scatter_recv, gather_send, gather_recv,
        spec_ssem, spec_rsem, edge_ssem, edge_rsem, sums_sem,
        image_out, grad_out, source_out, out_sem,
    ) = refs[3 + 2 * count :]
    me = lax.axis_index("src")
    tile = lax.axis_index("tile")
    other = 1 - tile

    own = pl.ds(pl.multiple_of(me * share, share), share)
    loads = {}

    def load(chosen):
        for i, name in enumerate(names):
            if name not in chosen:
                continue
            source = hbm[name]
            if name == "amb_back":
                source = source.at[tile, own]
            elif name == "row_amb":
                source = source.at[tile]
            elif name in OWN_ROWS:
                source = source.at[own]
            loads[name] = pltpu.make_async_copy(source, vmem[name], load_sem.at[i])
            loads[name].start()

    load(FIRST)
    barrier = pltpu.get_barrier_semaphore()
    for step in range(n):
        peer = lax.rem(me + step, n)
        if step:
            pl.semaphore_signal(barrier, inc=1, device_id={"src": peer, "tile": tile})
        pl.semaphore_signal(barrier, inc=1, device_id={"src": peer, "tile": other})

    load(SECOND)

    def table(name):
        loads[name].wait()
        return vmem[name][...]

    partial[...] = dot(table("mask"), table("col_fwd")).astype(jnp.bfloat16)
    pl.semaphore_wait(barrier, 2 * n - 1)
    rim = pl.ds(pl.multiple_of(other * (th - AMB), ROWS_16), AMB)
    halo_copy = pltpu.make_async_remote_copy(
        src_ref=partial.at[rim], dst_ref=halo, send_sem=halo_sem.at[0], recv_sem=halo_sem.at[1],
        device_id={"tile": other},
    )
    halo_copy.start()
    load([name for name in names if name not in FIRST + SECOND])

    for name in SCALARS + ("jones",):
        loads[name].wait()
    jones = vmem["jones"]
    lane = lax.broadcasted_iota(jnp.int32, (K, LANES), 1)
    left = lane < K
    for s in range(local):
        first, second, state = offsets[0, s], offsets[1, s], ids[s]
        low = lax.rem(LANES - second, LANES)
        high = K - second
        vec = [[polar[c, i, state] for i in range(2)] for c in range(2)]
        for j in range(3):
            win = [
                [jones[(c * 3 + j) * 2 + i, pl.ds(first, K), :] for i in range(2)]
                for c in range(2)
            ]
            real = sum(win[0][i] * vec[0][i] - win[1][i] * vec[1][i] for i in range(2))
            imag = sum(win[0][i] * vec[1][i] + win[1][i] * vec[0][i] for i in range(2))
            rows = slice((s * 3 + j) * K, (s * 3 + j + 1) * K)
            for value, kept in ((real, pupil_a), (imag, pupil_b)):
                kept[rows] = jnp.where(
                    left, pltpu.roll(value, low, 1), pltpu.roll(value, high, 1)
                )

    product = dot(table("row_fwd"), partial[...])

    halo_copy.wait()
    product = product + dot(table("row_amb"), halo[...])
    sign = jnp.where(left, 1.0, -1.0)
    norm = 1.0 / math.sqrt((th + 2 * AMB) * tw)
    spec = norm * (product[:K] + sign * pltpu.roll(product[K:], K, 1))
    turned = -sign * pltpu.roll(spec, K, 1)

    fields = 3 * local
    masked = [
        pupil_a[q * K : (q + 1) * K] * spec + pupil_b[q * K : (q + 1) * K] * turned
        for q in range(fields)
    ]
    cols = dot(jnp.concatenate(masked, 0).astype(jnp.bfloat16), table("col_inv"))
    cols = cols.astype(jnp.bfloat16)
    mixed = [
        jnp.concatenate([cols[q * K : (q + 1) * K, :grid], cols[q * K : (q + 1) * K, grid:]], 0)
        for q in range(fields)
    ]
    field[...] = dot(table("row_inv"), jnp.concatenate(mixed, 1))
    total = jnp.zeros((grid, grid), jnp.float32)
    for s in range(local):
        power_s = jnp.zeros((grid, grid), jnp.float32)
        for q in range(3 * s, 3 * s + 3):
            values = field[:, q * grid : (q + 1) * grid]
            power_s = power_s + values[:grid] * values[:grid] + values[grid:] * values[grid:]
        power[s] = power_s
        total = total + (weights[s] / parts_total) * power_s
    part[...] = total.astype(jnp.bfloat16)

    def block(index):
        return pl.ds(pl.multiple_of(index * block_rows, block_rows), block_rows)

    def guarded(condition, run):
        if owners == n:
            run()
        else:
            pl.when(condition)(run)

    scatter, gather = {}, {}
    for step in range(1, n):
        peer = lax.rem(me + step, n)
        to = peer if owners == n else jnp.minimum(peer, owners - 1)
        scatter[step] = pltpu.make_async_remote_copy(
            src_ref=part.at[block(to)], dst_ref=landed.at[step],
            send_sem=scatter_send.at[step], recv_sem=scatter_recv.at[step],
            device_id={"src": peer},
        )
        guarded(peer < owners, scatter[step].start)
    mine = me if owners == n else jnp.minimum(me, owners - 1)

    def reduce_own():
        acc = part[block(mine), :].astype(jnp.float32)
        for step in range(1, n):
            scatter[step].wait_recv()
            acc = acc + landed[step].astype(jnp.float32)
        reduced[...] = acc.astype(jnp.bfloat16)
        for step in range(1, n):
            gather[step].start()
        whole[block(mine), :] = reduced[...]

    for step in range(1, n):
        peer = lax.rem(me + step, n)
        gather[step] = pltpu.make_async_remote_copy(
            src_ref=reduced, dst_ref=whole.at[block(mine)],
            send_sem=gather_send.at[step], recv_sem=gather_recv.at[step],
            device_id={"src": peer},
        )
    projected = dot(table("target").astype(jnp.bfloat16), table("d_col_t")).astype(jnp.bfloat16)
    target_small[...] = dot(table("d_row_t"), projected)

    guarded(me < owners, reduce_own)
    row_inv_t = table("row_inv_t")
    col_back = table("col_back")
    gram = table("gram")
    for step in range(1, n):
        origin = lax.rem(me + n - step, n)
        guarded(origin < owners, gather[step].wait_recv)

    image = whole[...]
    twice = jnp.concatenate([image, image], 0)
    residual = dot(gram, twice) - target_small[...]
    doubled = jnp.concatenate([residual, residual], 0)

    scaled = [
        (doubled * field[:, q * grid : (q + 1) * grid]).astype(jnp.bfloat16) for q in range(fields)
    ]
    rows = dot(row_inv_t, jnp.concatenate(scaled, 1)).astype(jnp.bfloat16)
    mixed = [
        jnp.concatenate([rows[:K, q * grid : (q + 1) * grid], rows[K:, q * grid : (q + 1) * grid]], 1)
        for q in range(fields)
    ]
    both = dot(jnp.concatenate(mixed, 0), col_back)
    grad = jnp.zeros((K, LANES), jnp.float32)
    scale = 2.0 / (parts_total * K)
    for s in range(local):
        own_grad = jnp.zeros((K, LANES), jnp.float32)
        for q in range(3 * s, 3 * s + 3):
            rows_q = slice(q * K, (q + 1) * K)
            pair = both[rows_q]
            own_grad = own_grad + pupil_a[rows_q] * pair[:, :LANES] + pupil_b[rows_q] * pair[:, LANES:]
        grad = grad + (scale * weights[s]) * own_grad
    spec_send[...] = (norm * grad).astype(jnp.bfloat16)

    spread, rims = {}, []
    for step in range(1, n):
        peer = lax.rem(me + step, n)
        spread[step] = pltpu.make_async_remote_copy(
            src_ref=spec_send, dst_ref=spec_land.at[step],
            send_sem=spec_ssem.at[step], recv_sem=spec_rsem.at[step],
            device_id={"src": peer},
        )
        spread[step].start()
    for e in range(edges):
        rims.append(
            pltpu.make_async_remote_copy(
                src_ref=spec_send, dst_ref=edge_land.at[me],
                send_sem=edge_ssem.at[e], recv_sem=edge_rsem.at[me],
                device_id={"src": e + tile * (n - edges), "tile": other},
            )
        )
        rims[-1].start()
    for s in range(local):
        sums[s : s + 1, :] = jnp.sum(residual * power[s], 0, keepdims=True)
    sums_copy = pltpu.make_async_remote_copy(
        src_ref=sums, dst_ref=sums_land, send_sem=sums_sem.at[0], recv_sem=sums_sem.at[1],
        device_id={"tile": other},
    )
    sums_copy.start()

    lines = dot(table("d_row"), twice)
    lines_high = lines.astype(jnp.bfloat16)
    lines_low = (lines - lines_high.astype(jnp.float32)).astype(jnp.bfloat16)
    image_out[...] = dot(jnp.concatenate([lines_high, lines_low], 1), table("d_col"))

    writes = [
        pltpu.make_async_copy(source, to, out_sem.at[i])
        for i, (source, to) in enumerate(zip((image_out, grad_out, source_out), outputs))
    ]
    writes[0].start()

    row_back, amb_back, col_fwd_t = table("row_back"), table("amb_back"), table("col_fwd_t")
    sums_copy.wait()
    both_sums = jnp.sum(sums[...] + sums_land[...], 1, keepdims=True) / (2 * th * tw)
    for s in range(local):
        source_out[s] = both_sums[s, 0]
    writes[2].start()

    def stack(value):
        return jnp.concatenate([value, -sign * pltpu.roll(value, K, 1)], 0).astype(jnp.bfloat16)

    summed = spec_send[...].astype(jnp.float32)
    for step in range(1, n):
        spread[step].wait_recv()
        summed = summed + spec_land[step].astype(jnp.float32)
    rows = dot(row_back, stack(summed))
    at_rim = jnp.where(tile == 0, me >= n - edges, me < edges)

    @pl.when(at_rim)
    def _():
        outer = jnp.zeros((K, LANES), jnp.float32)
        for d in range(n):
            pltpu.make_async_remote_copy(
                src_ref=spec_send, dst_ref=edge_land.at[d],
                send_sem=edge_ssem.at[0], recv_sem=edge_rsem.at[d],
                device_id={"tile": other},
            ).wait_recv()
            outer = outer + edge_land[d].astype(jnp.float32)
        full = rows + dot(amb_back, stack(outer))
        grad_out[...] = GRAD_SCALE * dot(full.astype(jnp.bfloat16), col_fwd_t)

    @pl.when(jnp.logical_not(at_rim))
    def _():
        grad_out[...] = GRAD_SCALE * dot(rows.astype(jnp.bfloat16), col_fwd_t)

    writes[1].start()
    for step in range(1, n):
        guarded(lax.rem(me + step, n) < owners, scatter[step].wait_send)
        guarded(me < owners, gather[step].wait_send)
        spread[step].wait_send()
    for copy in rims:
        copy.wait_send()
    for copy in writes:
        copy.wait()


def write_outputs(image, grad, source, image_out, grad_out, source_out, held, scalars, sem):
    ways = [
        (image, held.at[0], image_out.at[0]),
        (grad, held.at[1], grad_out.at[0]),
        (source, scalars, source_out),
    ]
    loads = [pltpu.make_async_copy(w[0], w[1], sem.at[0, i]) for i, w in enumerate(ways)]
    stores = [pltpu.make_async_copy(w[1], w[2], sem.at[1, i]) for i, w in enumerate(ways)]
    for load in loads:
        load.start()
    for load, store in zip(loads, stores):
        load.wait()
        store.start()
    for store in stores:
        store.wait()


def body(
    mask_values, target_image, jones_pupil, polar_states, source_weights, pupil_offsets, polar_ids
):
    th, tw = mask_values.shape
    n = lax.axis_size("src")
    assert lax.axis_size("tile") == 2
    local = source_weights.shape[0]
    share = th // n
    grid = 2 * K
    owners = min(n, grid // ROWS_16)
    block_rows = grid // owners
    assert owners * block_rows == grid
    edges = -(-AMB // share)
    named = dict(
        mask=mask_values,
        target=target_image,
        jones=jones_pupil.reshape((-1,) + jones_pupil.shape[-2:]),
        offsets=pupil_offsets.T,
        ids=polar_ids,
        weights=source_weights,
        polar=polar_states.transpose(1, 2, 0),
    )
    constants = tables(th, tw)
    order = ["mask", "col_fwd", *SCALARS, "jones", "row_fwd", "target", "d_col_t", "d_row_t"]
    order += [name for name in constants if name not in order]
    arrays = []
    held = []
    for name in order:
        value = named[name] if name in named else jnp.asarray(constants[name])
        arrays.append(value)
        shape = value.shape
        if name == "amb_back":
            shape = (share,) + shape[2:]
        elif name == "row_amb":
            shape = shape[1:]
        elif name in OWN_ROWS:
            shape = (share,) + shape[1:]
        held.append((pltpu.SMEM if name in SCALARS else pltpu.VMEM)(shape, value.dtype))
    f32, bf16 = jnp.float32, jnp.bfloat16
    sems = pltpu.SemaphoreType.DMA
    scratch = held + [
        pltpu.VMEM((th, LANES), bf16),
        pltpu.VMEM((AMB, LANES), bf16),
        pltpu.VMEM((3 * local * K, LANES), f32),
        pltpu.VMEM((3 * local * K, LANES), f32),
        pltpu.VMEM((2 * grid, 3 * local * grid), f32),
        pltpu.VMEM((local, grid, grid), f32),
        pltpu.VMEM((grid, grid), f32),
        pltpu.VMEM((grid, grid), bf16),
        pltpu.VMEM((n, block_rows, grid), bf16),
        pltpu.VMEM((block_rows, grid), bf16),
        pltpu.VMEM((grid, grid), bf16),
        pltpu.VMEM((K, LANES), bf16),
        pltpu.VMEM((n, K, LANES), bf16),
        pltpu.VMEM((n, K, LANES), bf16),
        pltpu.VMEM((local, LANES), f32),
        pltpu.VMEM((local, LANES), f32),
        sems((len(order),)),
        sems((2,)),
        sems((n,)),
        sems((n,)),
        sems((n,)),
        sems((n,)),
        sems((n,)),
        sems((n,)),
        sems((edges,)),
        sems((n,)),
        sems((2,)),
        pltpu.VMEM((share, tw), f32),
        pltpu.VMEM((share, tw), f32),
        pltpu.SMEM((local,), f32),
        sems((3,)),
    ]
    sizes = (n, local, th, tw, share, owners, block_rows, edges, local * n)
    in_hbm = pl.BlockSpec(memory_space=pltpu.HBM)
    results = pl.pallas_call(
        functools.partial(kernel, tuple(order), sizes),
        out_shape=(
            jax.ShapeDtypeStruct((share, tw), f32),
            jax.ShapeDtypeStruct((share, tw), f32),
            jax.ShapeDtypeStruct((local,), f32),
        ),
        in_specs=[in_hbm] * len(arrays),
        out_specs=(in_hbm,) * 3,
        scratch_shapes=scratch,
        compiler_params=pltpu.CompilerParams(
            collective_id=0, has_side_effects=True, vmem_limit_bytes=VMEM_LIMIT
        ),
    )(*arrays)
    return pl.pallas_call(
        write_outputs,
        out_shape=(
            jax.ShapeDtypeStruct((1, share, tw), f32),
            jax.ShapeDtypeStruct((1, share, tw), f32),
            jax.ShapeDtypeStruct((local,), f32),
        ),
        in_specs=[in_hbm] * 3,
        out_specs=(in_hbm,) * 3,
        scratch_shapes=[pltpu.VMEM((2, share, tw), f32), pltpu.SMEM((local,), f32), sems((2, 3))],
        compiler_params=pltpu.CompilerParams(vmem_limit_bytes=VMEM_LIMIT),
    )(*results)


def solution(mesh):
    placed = (
        P(("parts", "tile"), None),
        P(("parts", "tile"), None),
        P(),
        P(),
        P(("parts", "src")),
        P(("parts", "src"), None),
        P(("parts", "src")),
    )
    return jax.shard_map(
        body,
        mesh=mesh,
        in_specs=placed,
        out_specs=(
            P(("parts", "tile"), "src", None),
            P(("parts", "tile"), "src", None),
            P(("parts", "src")),
        ),
        check_vma=False,
    )
```

```python
import functools
import math

import jax
import jax.numpy as jnp
import ml_dtypes
import numpy as np
from jax import lax
from jax.experimental import pallas as pl
from jax.experimental.pallas import tpu as pltpu
from jax.sharding import PartitionSpec as P

AMB = 64
K = 64
GRAD_SCALE = 32.0
LANES = 2 * K
VMEM_LIMIT = 64 * 1024 * 1024 - 512 * 1024
ROWS_16 = 16


def split_bf16(table):
    high = table.astype(ml_dtypes.bfloat16)
    low = (table - high.astype(np.float64)).astype(ml_dtypes.bfloat16)
    return high, low


def tables(th, tw):
    window = th + 2 * AMB
    grid = 2 * K
    orders = np.arange(K) - K // 2
    diffs = np.arange(-(K - 1), K)

    def angle(left, right, period):
        return 2.0 * np.pi * np.mod(np.outer(left, right), period) / period

    bf = lambda x: np.ascontiguousarray(x).astype(ml_dtypes.bfloat16)
    col = angle(np.arange(tw), orders, tw)
    col_fwd = np.concatenate([np.cos(col), -np.sin(col)], 1)
    row = angle(orders, np.arange(window), window)
    row_fwd = np.concatenate([np.cos(row), np.sin(row)], 0)
    row_amb = np.stack([row_fwd[:, th + AMB :], row_fwd[:, :AMB]])
    row_back = row_fwd[:, AMB : AMB + th].T
    amb_back = np.zeros((2, th, 2 * K))
    amb_back[0, th - AMB :] = row_fwd[:, :AMB].T
    amb_back[1, :AMB] = row_fwd[:, th + AMB :].T
    small = angle(np.arange(grid), orders, grid)
    cos, sin = np.cos(small), np.sin(small)
    row_inv = np.concatenate(
        [np.concatenate([cos, -sin], 1), np.concatenate([sin, cos], 1)], 0
    )
    col_inv = np.concatenate(
        [np.concatenate([cos.T, sin.T], 1), np.concatenate([-sin.T, cos.T], 1)], 0
    )
    back = col_inv.T
    col_back = np.concatenate([back, back[:, K:], -back[:, :K]], 1)

    def dirichlet(positions):
        turn = positions[:, None] - np.arange(grid)[None, :] / grid
        return np.cos(2.0 * np.pi * turn[:, :, None] * diffs).sum(-1) / grid

    d_row = dirichlet((np.arange(th) + AMB) / window)
    d_col = dirichlet(np.arange(tw) / tw)
    gram = (tw / grid) * (d_row.T @ d_row)
    cat = lambda *parts: np.concatenate(parts, 1)
    wide_early = cat(bf(row_fwd[:, AMB : AMB + th]), bf(col_inv / K))
    wide_late = cat(bf(d_row.T), *split_bf16(gram), bf(row_inv.T), bf(col_fwd.T))
    tall_late = cat(bf(col_back), bf(np.concatenate([d_col.T, d_col.T], 0)))
    own_rows = cat(*split_bf16(d_row), bf(row_back))
    return dict(
        col_fwd=bf(col_fwd),
        wide_early=wide_early,
        row_amb=bf(row_amb),
        row_inv=bf(row_inv),
        d_col_t=bf(d_col),
        wide_late=wide_late,
        tall_late=tall_late,
        own_rows=own_rows,
        amb_back=bf(amb_back),
    )


SCALARS = ("offsets", "ids", "weights", "polar")
FIRST = ("rim", "col_fwd", "mask")


def dot(a, b):
    return jnp.dot(a, b, preferred_element_type=jnp.float32)


def kernel(names, sizes, *refs):
    n, local, th, tw, share, owners, block_rows, edges, parts_total = sizes
    grid = 2 * K
    count = len(names)
    hbm = dict(zip(names, refs[:count]))
    outputs = refs[count : 3 + count]
    vmem = dict(zip(names, refs[3 + count : 3 + 2 * count]))
    offsets, ids, weights, polar = (vmem[name] for name in SCALARS)
    (
        rim_rows, rim_send, halo, pupil_a, pupil_b, field, power, target_small,
        part, landed, reduced, whole, spec_send, spec_land, edge_land, sums, sums_land,
        load_sem, halo_sem, scatter_send, scatter_recv, gather_send, gather_recv,
        spec_ssem, spec_rsem, edge_ssem, edge_rsem, sums_sem,
        image_out, grad_out, source_out, out_sem,
    ) = refs[3 + 2 * count :]
    me = lax.axis_index("src")
    tile = lax.axis_index("tile")
    other = 1 - tile

    own = pl.ds(pl.multiple_of(me * share, share), share)
    rim = pl.ds(pl.multiple_of(other * (th - AMB), ROWS_16), AMB)
    parts_of = {
        "rim": lambda ref: ref.at[rim],
        "amb_back": lambda ref: ref.at[tile, own],
        "row_amb": lambda ref: ref.at[tile],
        "own_rows": lambda ref: ref.at[own],
    }
    loads = {}

    def load(chosen):
        for name in chosen:
            source = hbm["mask" if name == "rim" else name]
            source = parts_of[name](source) if name in parts_of else source
            target = rim_rows if name == "rim" else vmem[name]
            loads[name] = pltpu.make_async_copy(source, target, load_sem.at[len(loads)])
            loads[name].start()

    load(FIRST)
    barrier = pltpu.get_barrier_semaphore()
    for step in range(n):
        peer = lax.rem(me + step, n)
        if step:
            pl.semaphore_signal(barrier, inc=1, device_id={"src": peer, "tile": tile})
        pl.semaphore_signal(barrier, inc=1, device_id={"src": peer, "tile": other})
    load([name for name in names if name not in FIRST])
    waited = set()

    def table(name, start=0, stop=None):
        if name not in waited:
            loads[name].wait()
            waited.add(name)
        return vmem[name][:, start:stop]

    loads["rim"].wait()
    rim_send[...] = dot(rim_rows[...], table("col_fwd")).astype(jnp.bfloat16)
    pl.semaphore_wait(barrier, 2 * n - 1)
    halo_copy = pltpu.make_async_remote_copy(
        src_ref=rim_send, dst_ref=halo, send_sem=halo_sem.at[0], recv_sem=halo_sem.at[1],
        device_id={"tile": other},
    )
    halo_copy.start()
    partial = dot(table("mask"), table("col_fwd")).astype(jnp.bfloat16)

    for name in SCALARS + ("jones",):
        loads[name].wait()
    jones = vmem["jones"]
    lane = lax.broadcasted_iota(jnp.int32, (K, LANES), 1)
    left = lane < K
    for s in range(local):
        first, second, state = offsets[0, s], offsets[1, s], ids[s]
        low = lax.rem(LANES - second, LANES)
        high = K - second
        vec = [[polar[c, i, state] for i in range(2)] for c in range(2)]
        for j in range(3):
            win = [
                [jones[(c * 3 + j) * 2 + i, pl.ds(first, K), :] for i in range(2)]
                for c in range(2)
            ]
            real = sum(win[0][i] * vec[0][i] - win[1][i] * vec[1][i] for i in range(2))
            imag = sum(win[0][i] * vec[1][i] + win[1][i] * vec[0][i] for i in range(2))
            rows = slice((s * 3 + j) * K, (s * 3 + j + 1) * K)
            for value, kept in ((real, pupil_a), (imag, pupil_b)):
                kept[rows] = jnp.where(
                    left, pltpu.roll(value, low, 1), pltpu.roll(value, high, 1)
                )

    product = dot(table("wide_early", 0, th), partial)

    halo_copy.wait()
    product = product + dot(table("row_amb"), halo[...])
    sign = jnp.where(left, 1.0, -1.0)
    norm = 1.0 / math.sqrt((th + 2 * AMB) * tw)
    spec = norm * (product[:K] + sign * pltpu.roll(product[K:], K, 1))
    turned = -sign * pltpu.roll(spec, K, 1)

    fields = 3 * local
    masked = [
        pupil_a[q * K : (q + 1) * K] * spec + pupil_b[q * K : (q + 1) * K] * turned
        for q in range(fields)
    ]
    cols = dot(jnp.concatenate(masked, 0).astype(jnp.bfloat16), table("wide_early", th))
    cols = cols.astype(jnp.bfloat16)
    mixed = [
        jnp.concatenate([cols[q * K : (q + 1) * K, :grid], cols[q * K : (q + 1) * K, grid:]], 0)
        for q in range(fields)
    ]
    field[...] = dot(table("row_inv"), jnp.concatenate(mixed, 1))
    total = jnp.zeros((grid, grid), jnp.float32)
    for s in range(local):
        power_s = jnp.zeros((grid, grid), jnp.float32)
        for q in range(3 * s, 3 * s + 3):
            values = field[:, q * grid : (q + 1) * grid]
            power_s = power_s + values[:grid] * values[:grid] + values[grid:] * values[grid:]
        power[s] = power_s
        total = total + (weights[s] / parts_total) * power_s
    part[...] = total.astype(jnp.bfloat16)

    def block(index):
        return pl.ds(pl.multiple_of(index * block_rows, block_rows), block_rows)

    def guarded(condition, run):
        if owners == n:
            run()
        else:
            pl.when(condition)(run)

    scatter, gather = {}, {}
    for step in range(1, n):
        peer = lax.rem(me + step, n)
        to = peer if owners == n else jnp.minimum(peer, owners - 1)
        scatter[step] = pltpu.make_async_remote_copy(
            src_ref=part.at[block(to)], dst_ref=landed.at[step],
            send_sem=scatter_send.at[step], recv_sem=scatter_recv.at[step],
            device_id={"src": peer},
        )
        guarded(peer < owners, scatter[step].start)
    mine = me if owners == n else jnp.minimum(me, owners - 1)

    def reduce_own():
        acc = part[block(mine), :].astype(jnp.float32)
        for step in range(1, n):
            scatter[step].wait_recv()
            acc = acc + landed[step].astype(jnp.float32)
        reduced[...] = acc.astype(jnp.bfloat16)
        for step in range(1, n):
            gather[step].start()
        whole[block(mine), :] = reduced[...]

    for step in range(1, n):
        peer = lax.rem(me + step, n)
        gather[step] = pltpu.make_async_remote_copy(
            src_ref=reduced, dst_ref=whole.at[block(mine)],
            send_sem=gather_send.at[step], recv_sem=gather_recv.at[step],
            device_id={"src": peer},
        )
    projected = dot(table("target").astype(jnp.bfloat16), table("d_col_t")).astype(jnp.bfloat16)
    target_small[...] = dot(table("wide_late", 0, th), projected)

    guarded(me < owners, reduce_own)
    row_inv_t = table("wide_late", th + 2 * grid, th + 4 * grid)
    col_back = table("tall_late", 0, 4 * K)
    gram = table("wide_late", th, th + 2 * grid)
    for step in range(1, n):
        origin = lax.rem(me + n - step, n)
        guarded(origin < owners, gather[step].wait_recv)

    image = whole[...]
    twice = jnp.concatenate([image, image], 0)
    residual = dot(gram, twice) - target_small[...]
    doubled = jnp.concatenate([residual, residual], 0)

    scaled = [
        (doubled * field[:, q * grid : (q + 1) * grid]).astype(jnp.bfloat16) for q in range(fields)
    ]
    rows = dot(row_inv_t, jnp.concatenate(scaled, 1)).astype(jnp.bfloat16)
    mixed = [
        jnp.concatenate([rows[:K, q * grid : (q + 1) * grid], rows[K:, q * grid : (q + 1) * grid]], 1)
        for q in range(fields)
    ]
    both = dot(jnp.concatenate(mixed, 0), col_back)
    grad = jnp.zeros((K, LANES), jnp.float32)
    scale = 2.0 / (parts_total * K)
    for s in range(local):
        own_grad = jnp.zeros((K, LANES), jnp.float32)
        for q in range(3 * s, 3 * s + 3):
            rows_q = slice(q * K, (q + 1) * K)
            pair = both[rows_q]
            own_grad = own_grad + pupil_a[rows_q] * pair[:, :LANES] + pupil_b[rows_q] * pair[:, LANES:]
        grad = grad + (scale * weights[s]) * own_grad
    spec_send[...] = (norm * grad).astype(jnp.bfloat16)

    spread, rims = {}, []
    for step in range(1, n):
        peer = lax.rem(me + step, n)
        spread[step] = pltpu.make_async_remote_copy(
            src_ref=spec_send, dst_ref=spec_land.at[step],
            send_sem=spec_ssem.at[step], recv_sem=spec_rsem.at[step],
            device_id={"src": peer},
        )
        spread[step].start()
    for e in range(edges):
        rims.append(
            pltpu.make_async_remote_copy(
                src_ref=spec_send, dst_ref=edge_land.at[me],
                send_sem=edge_ssem.at[e], recv_sem=edge_rsem.at[me],
                device_id={"src": e + tile * (n - edges), "tile": other},
            )
        )
        rims[-1].start()
    for s in range(local):
        sums[s : s + 1, :] = jnp.sum(residual * power[s], 0, keepdims=True)
    sums_copy = pltpu.make_async_remote_copy(
        src_ref=sums, dst_ref=sums_land, send_sem=sums_sem.at[0], recv_sem=sums_sem.at[1],
        device_id={"tile": other},
    )
    sums_copy.start()

    lines = dot(table("own_rows", 0, 2 * grid), twice)
    lines_high = lines.astype(jnp.bfloat16)
    lines_low = (lines - lines_high.astype(jnp.float32)).astype(jnp.bfloat16)
    image_out[...] = dot(jnp.concatenate([lines_high, lines_low], 1), table("tall_late", 4 * K))

    writes = [
        pltpu.make_async_copy(source, to, out_sem.at[i])
        for i, (source, to) in enumerate(zip((image_out, grad_out, source_out), outputs))
    ]
    writes[0].start()

    row_back, amb_back = table("own_rows", 2 * grid), table("amb_back")
    col_fwd_t = table("wide_late", th + 4 * grid)
    sums_copy.wait()
    both_sums = jnp.sum(sums[...] + sums_land[...], 1, keepdims=True) / (2 * th * tw)
    for s in range(local):
        source_out[s] = both_sums[s, 0]
    writes[2].start()

    def stack(value):
        return jnp.concatenate([value, -sign * pltpu.roll(value, K, 1)], 0).astype(jnp.bfloat16)

    summed = spec_send[...].astype(jnp.float32)
    for step in range(1, n):
        spread[step].wait_recv()
        summed = summed + spec_land[step].astype(jnp.float32)
    rows = dot(row_back, stack(summed))
    at_rim = jnp.where(tile == 0, me >= n - edges, me < edges)

    @pl.when(at_rim)
    def _():
        outer = jnp.zeros((K, LANES), jnp.float32)
        for d in range(n):
            pltpu.make_async_remote_copy(
                src_ref=spec_send, dst_ref=edge_land.at[d],
                send_sem=edge_ssem.at[0], recv_sem=edge_rsem.at[d],
                device_id={"tile": other},
            ).wait_recv()
            outer = outer + edge_land[d].astype(jnp.float32)
        full = rows + dot(amb_back, stack(outer))
        grad_out[...] = GRAD_SCALE * dot(full.astype(jnp.bfloat16), col_fwd_t)

    @pl.when(jnp.logical_not(at_rim))
    def _():
        grad_out[...] = GRAD_SCALE * dot(rows.astype(jnp.bfloat16), col_fwd_t)

    writes[1].start()
    for step in range(1, n):
        guarded(lax.rem(me + step, n) < owners, scatter[step].wait_send)
        guarded(me < owners, gather[step].wait_send)
        spread[step].wait_send()
    for copy in rims:
        copy.wait_send()
    for copy in writes:
        copy.wait()


def write_outputs(image, grad, source, image_out, grad_out, source_out, held, scalars, sem):
    ways = [
        (image, held.at[0], image_out.at[0]),
        (grad, held.at[1], grad_out.at[0]),
        (source, scalars, source_out),
    ]
    loads = [pltpu.make_async_copy(w[0], w[1], sem.at[0, i]) for i, w in enumerate(ways)]
    stores = [pltpu.make_async_copy(w[1], w[2], sem.at[1, i]) for i, w in enumerate(ways)]
    for load in loads:
        load.start()
    for load, store in zip(loads, stores):
        load.wait()
        store.start()
    for store in stores:
        store.wait()


def body(
    mask_values, target_image, jones_pupil, polar_states, source_weights, pupil_offsets, polar_ids
):
    th, tw = mask_values.shape
    n = lax.axis_size("src")
    assert lax.axis_size("tile") == 2
    local = source_weights.shape[0]
    share = th // n
    grid = 2 * K
    owners = min(n, grid // ROWS_16)
    block_rows = grid // owners
    assert owners * block_rows == grid
    edges = -(-AMB // share)
    named = dict(
        mask=mask_values,
        target=target_image,
        jones=jones_pupil.reshape((-1,) + jones_pupil.shape[-2:]),
        offsets=pupil_offsets.T,
        ids=polar_ids,
        weights=source_weights,
        polar=polar_states.transpose(1, 2, 0),
    )
    constants = tables(th, tw)
    order = ["mask", "col_fwd", *SCALARS, "jones", "wide_early", "row_amb", "row_inv", "target"]
    order += [name for name in constants if name not in order]
    arrays = []
    held = []
    for name in order:
        value = named[name] if name in named else jnp.asarray(constants[name])
        arrays.append(value)
        shape = value.shape
        if name == "amb_back":
            shape = (share,) + shape[2:]
        elif name == "row_amb":
            shape = shape[1:]
        elif name == "own_rows":
            shape = (share,) + shape[1:]
        held.append((pltpu.SMEM if name in SCALARS else pltpu.VMEM)(shape, value.dtype))
    f32, bf16 = jnp.float32, jnp.bfloat16
    sems = pltpu.SemaphoreType.DMA
    scratch = held + [
        pltpu.VMEM((AMB, tw), bf16),
        pltpu.VMEM((AMB, LANES), bf16),
        pltpu.VMEM((AMB, LANES), bf16),
        pltpu.VMEM((3 * local * K, LANES), f32),
        pltpu.VMEM((3 * local * K, LANES), f32),
        pltpu.VMEM((2 * grid, 3 * local * grid), f32),
        pltpu.VMEM((local, grid, grid), f32),
        pltpu.VMEM((grid, grid), f32),
        pltpu.VMEM((grid, grid), bf16),
        pltpu.VMEM((n, block_rows, grid), bf16),
        pltpu.VMEM((block_rows, grid), bf16),
        pltpu.VMEM((grid, grid), bf16),
        pltpu.VMEM((K, LANES), bf16),
        pltpu.VMEM((n, K, LANES), bf16),
        pltpu.VMEM((n, K, LANES), bf16),
        pltpu.VMEM((local, LANES), f32),
        pltpu.VMEM((local, LANES), f32),
        sems((len(order) + 1,)),
        sems((2,)),
        sems((n,)),
        sems((n,)),
        sems((n,)),
        sems((n,)),
        sems((n,)),
        sems((n,)),
        sems((edges,)),
        sems((n,)),
        sems((2,)),
        pltpu.VMEM((share, tw), f32),
        pltpu.VMEM((share, tw), f32),
        pltpu.SMEM((local,), f32),
        sems((3,)),
    ]
    sizes = (n, local, th, tw, share, owners, block_rows, edges, local * n)
    in_hbm = pl.BlockSpec(memory_space=pltpu.HBM)
    results = pl.pallas_call(
        functools.partial(kernel, tuple(order), sizes),
        out_shape=(
            jax.ShapeDtypeStruct((share, tw), f32),
            jax.ShapeDtypeStruct((share, tw), f32),
            jax.ShapeDtypeStruct((local,), f32),
        ),
        in_specs=[in_hbm] * len(arrays),
        out_specs=(in_hbm,) * 3,
        scratch_shapes=scratch,
        compiler_params=pltpu.CompilerParams(
            collective_id=0, has_side_effects=True, vmem_limit_bytes=VMEM_LIMIT
        ),
    )(*arrays)
    return pl.pallas_call(
        write_outputs,
        out_shape=(
            jax.ShapeDtypeStruct((1, share, tw), f32),
            jax.ShapeDtypeStruct((1, share, tw), f32),
            jax.ShapeDtypeStruct((local,), f32),
        ),
        in_specs=[in_hbm] * 3,
        out_specs=(in_hbm,) * 3,
        scratch_shapes=[pltpu.VMEM((2, share, tw), f32), pltpu.SMEM((local,), f32), sems((2, 3))],
        compiler_params=pltpu.CompilerParams(vmem_limit_bytes=VMEM_LIMIT),
    )(*results)


def solution(mesh):
    placed = (
        P(("parts", "tile"), None),
        P(("parts", "tile"), None),
        P(),
        P(),
        P(("parts", "src")),
        P(("parts", "src"), None),
        P(("parts", "src")),
    )
    return jax.shard_map(
        body,
        mesh=mesh,
        in_specs=placed,
        out_specs=(
            P(("parts", "tile"), "src", None),
            P(("parts", "tile"), "src", None),
            P(("parts", "src")),
        ),
        check_vma=False,
    )
```

```python
import functools
import math

import jax
import jax.numpy as jnp
import ml_dtypes
import numpy as np
from jax import lax
from jax.experimental import pallas as pl
from jax.experimental.pallas import tpu as pltpu
from jax.sharding import PartitionSpec as P

AMB = 64
K = 64
GRAD_SCALE = 32.0
LANES = 2 * K
VMEM_LIMIT = 64 * 1024 * 1024 - 512 * 1024
ROWS_16 = 16


def split_bf16(table):
    high = table.astype(ml_dtypes.bfloat16)
    low = (table - high.astype(np.float64)).astype(ml_dtypes.bfloat16)
    return high, low


def tables(th, tw):
    window = th + 2 * AMB
    grid = 2 * K
    orders = np.arange(K) - K // 2
    diffs = np.arange(-(K - 1), K)

    def angle(left, right, period):
        return 2.0 * np.pi * np.mod(np.outer(left, right), period) / period

    bf = lambda x: np.ascontiguousarray(x).astype(ml_dtypes.bfloat16)
    col = angle(np.arange(tw), orders, tw)
    col_fwd = np.concatenate([np.cos(col), -np.sin(col)], 1)
    row = angle(orders, np.arange(window), window)
    row_fwd = np.concatenate([np.cos(row), np.sin(row)], 0)
    row_amb = np.stack([row_fwd[:, th + AMB :], row_fwd[:, :AMB]])
    row_back = row_fwd[:, AMB : AMB + th].T
    amb_back = np.zeros((2, th, 2 * K))
    amb_back[0, th - AMB :] = row_fwd[:, :AMB].T
    amb_back[1, :AMB] = row_fwd[:, th + AMB :].T
    small = angle(np.arange(grid), orders, grid)
    cos, sin = np.cos(small), np.sin(small)
    row_inv = np.concatenate(
        [np.concatenate([cos, -sin], 1), np.concatenate([sin, cos], 1)], 0
    )
    col_inv = np.concatenate(
        [np.concatenate([cos.T, sin.T], 1), np.concatenate([-sin.T, cos.T], 1)], 0
    )
    back = col_inv.T
    col_back = np.concatenate([back, back[:, K:], -back[:, :K]], 1)

    def dirichlet(positions):
        turn = positions[:, None] - np.arange(grid)[None, :] / grid
        return np.cos(2.0 * np.pi * turn[:, :, None] * diffs).sum(-1) / grid

    d_row = dirichlet((np.arange(th) + AMB) / window)
    d_col = dirichlet(np.arange(tw) / tw)
    gram = (tw / grid) * (d_row.T @ d_row)
    cat = lambda *parts: np.concatenate(parts, 1)
    wide_early = cat(bf(row_fwd[:, AMB : AMB + th]), bf(col_inv / K))
    wide_late = cat(bf(d_row.T), *split_bf16(gram), bf(row_inv.T), bf(col_fwd.T))
    tall_late = cat(bf(col_back), bf(np.concatenate([d_col.T, d_col.T], 0)))
    own_rows = cat(*split_bf16(d_row), bf(row_back))
    return dict(
        col_fwd=bf(col_fwd),
        wide_early=wide_early,
        row_amb=bf(row_amb),
        row_inv=bf(row_inv),
        d_col_t=bf(d_col),
        wide_late=wide_late,
        tall_late=tall_late,
        own_rows=own_rows,
        amb_back=bf(amb_back),
    )


SCALARS = ("offsets", "ids", "weights", "polar")
FIRST = ("rim", "col_fwd", "mask")


def dot(a, b):
    return jnp.dot(a, b, preferred_element_type=jnp.float32)


def kernel(names, sizes, *refs):
    n, local, th, tw, share, owners, block_rows, edges, parts_total = sizes
    grid = 2 * K
    count = len(names)
    hbm = dict(zip(names, refs[:count]))
    outputs = refs[count : 3 + count]
    vmem = dict(zip(names, refs[3 + count : 3 + 2 * count]))
    offsets, ids, weights, polar = (vmem[name] for name in SCALARS)
    (
        rim_rows, rim_send, halo, pupil_a, pupil_b, field, power, target_small,
        part, landed, reduced, whole, spec_send, spec_land, spec_half, half_land, sums, sums_land,
        load_sem, halo_sem, scatter_send, scatter_recv, gather_send, gather_recv,
        spec_ssem, spec_rsem, edge_ssem, edge_rsem, sums_sem,
        image_out, grad_out, source_out, out_sem,
    ) = refs[3 + 2 * count :]
    me = lax.axis_index("src")
    tile = lax.axis_index("tile")
    other = 1 - tile

    own = pl.ds(pl.multiple_of(me * share, share), share)
    rim = pl.ds(pl.multiple_of(other * (th - AMB), ROWS_16), AMB)
    parts_of = {
        "rim": lambda ref: ref.at[rim],
        "amb_back": lambda ref: ref.at[tile, own],
        "row_amb": lambda ref: ref.at[tile],
        "own_rows": lambda ref: ref.at[own],
    }
    loads = {}

    def load(chosen):
        for name in chosen:
            source = hbm["mask" if name == "rim" else name]
            source = parts_of[name](source) if name in parts_of else source
            target = rim_rows if name == "rim" else vmem[name]
            loads[name] = pltpu.make_async_copy(source, target, load_sem.at[len(loads)])
            loads[name].start()

    load(FIRST)
    barrier = pltpu.get_barrier_semaphore()
    half = n // 2
    twin = lax.rem(me + half, n)
    for step in range(1, n):
        peer = lax.rem(me + step, n)
        pl.semaphore_signal(barrier, inc=1, device_id={"src": peer, "tile": tile})
    for peer in (me, twin):
        pl.semaphore_signal(barrier, inc=1, device_id={"src": peer, "tile": other})
    load([name for name in names if name not in FIRST])
    waited = set()

    def table(name, start=0, stop=None):
        if name not in waited:
            loads[name].wait()
            waited.add(name)
        return vmem[name][:, start:stop]

    loads["rim"].wait()
    rim_send[...] = dot(rim_rows[...], table("col_fwd")).astype(jnp.bfloat16)
    pl.semaphore_wait(barrier, n + 1)
    halo_copy = pltpu.make_async_remote_copy(
        src_ref=rim_send, dst_ref=halo, send_sem=halo_sem.at[0], recv_sem=halo_sem.at[1],
        device_id={"tile": other},
    )
    halo_copy.start()
    partial = dot(table("mask"), table("col_fwd")).astype(jnp.bfloat16)

    for name in SCALARS + ("jones",):
        loads[name].wait()
    jones = vmem["jones"]
    lane = lax.broadcasted_iota(jnp.int32, (K, LANES), 1)
    left = lane < K
    for s in range(local):
        first, second, state = offsets[0, s], offsets[1, s], ids[s]
        low = lax.rem(LANES - second, LANES)
        high = K - second
        vec = [[polar[c, i, state] for i in range(2)] for c in range(2)]
        for j in range(3):
            win = [
                [jones[(c * 3 + j) * 2 + i, pl.ds(first, K), :] for i in range(2)]
                for c in range(2)
            ]
            real = sum(win[0][i] * vec[0][i] - win[1][i] * vec[1][i] for i in range(2))
            imag = sum(win[0][i] * vec[1][i] + win[1][i] * vec[0][i] for i in range(2))
            rows = slice((s * 3 + j) * K, (s * 3 + j + 1) * K)
            for value, kept in ((real, pupil_a), (imag, pupil_b)):
                kept[rows] = jnp.where(
                    left, pltpu.roll(value, low, 1), pltpu.roll(value, high, 1)
                )

    product = dot(table("wide_early", 0, th), partial)

    halo_copy.wait()
    product = product + dot(table("row_amb"), halo[...])
    sign = jnp.where(left, 1.0, -1.0)
    norm = 1.0 / math.sqrt((th + 2 * AMB) * tw)
    spec = norm * (product[:K] + sign * pltpu.roll(product[K:], K, 1))
    turned = -sign * pltpu.roll(spec, K, 1)

    fields = 3 * local
    masked = [
        pupil_a[q * K : (q + 1) * K] * spec + pupil_b[q * K : (q + 1) * K] * turned
        for q in range(fields)
    ]
    cols = dot(jnp.concatenate(masked, 0).astype(jnp.bfloat16), table("wide_early", th))
    cols = cols.astype(jnp.bfloat16)
    mixed = [
        jnp.concatenate([cols[q * K : (q + 1) * K, :grid], cols[q * K : (q + 1) * K, grid:]], 0)
        for q in range(fields)
    ]
    field[...] = dot(table("row_inv"), jnp.concatenate(mixed, 1))
    total = jnp.zeros((grid, grid), jnp.float32)
    for s in range(local):
        power_s = jnp.zeros((grid, grid), jnp.float32)
        for q in range(3 * s, 3 * s + 3):
            values = field[:, q * grid : (q + 1) * grid]
            power_s = power_s + values[:grid] * values[:grid] + values[grid:] * values[grid:]
        power[s] = power_s
        total = total + (weights[s] / parts_total) * power_s
    part[...] = total.astype(jnp.bfloat16)

    def block(index):
        return pl.ds(pl.multiple_of(index * block_rows, block_rows), block_rows)

    def guarded(condition, run):
        if owners == n:
            run()
        else:
            pl.when(condition)(run)

    scatter, gather = {}, {}
    for step in range(1, n):
        peer = lax.rem(me + step, n)
        to = peer if owners == n else jnp.minimum(peer, owners - 1)
        scatter[step] = pltpu.make_async_remote_copy(
            src_ref=part.at[block(to)], dst_ref=landed.at[step],
            send_sem=scatter_send.at[step], recv_sem=scatter_recv.at[step],
            device_id={"src": peer},
        )
        guarded(peer < owners, scatter[step].start)
    mine = me if owners == n else jnp.minimum(me, owners - 1)

    def reduce_own():
        acc = part[block(mine), :].astype(jnp.float32)
        for step in range(1, n):
            scatter[step].wait_recv()
            acc = acc + landed[step].astype(jnp.float32)
        reduced[...] = acc.astype(jnp.bfloat16)
        for step in range(1, n):
            gather[step].start()
        whole[block(mine), :] = reduced[...]

    for step in range(1, n):
        peer = lax.rem(me + step, n)
        gather[step] = pltpu.make_async_remote_copy(
            src_ref=reduced, dst_ref=whole.at[block(mine)],
            send_sem=gather_send.at[step], recv_sem=gather_recv.at[step],
            device_id={"src": peer},
        )
    projected = dot(table("target").astype(jnp.bfloat16), table("d_col_t")).astype(jnp.bfloat16)
    target_small[...] = dot(table("wide_late", 0, th), projected)

    guarded(me < owners, reduce_own)
    row_inv_t = table("wide_late", th + 2 * grid, th + 4 * grid)
    col_back = table("tall_late", 0, 4 * K)
    gram = table("wide_late", th, th + 2 * grid)
    for step in range(1, n):
        origin = lax.rem(me + n - step, n)
        guarded(origin < owners, gather[step].wait_recv)

    image = whole[...]
    twice = jnp.concatenate([image, image], 0)
    residual = dot(gram, twice) - target_small[...]
    doubled = jnp.concatenate([residual, residual], 0)

    scaled = [
        (doubled * field[:, q * grid : (q + 1) * grid]).astype(jnp.bfloat16) for q in range(fields)
    ]
    rows = dot(row_inv_t, jnp.concatenate(scaled, 1)).astype(jnp.bfloat16)
    mixed = [
        jnp.concatenate([rows[:K, q * grid : (q + 1) * grid], rows[K:, q * grid : (q + 1) * grid]], 1)
        for q in range(fields)
    ]
    both = dot(jnp.concatenate(mixed, 0), col_back)
    grad = jnp.zeros((K, LANES), jnp.float32)
    scale = 2.0 / (parts_total * K)
    for s in range(local):
        own_grad = jnp.zeros((K, LANES), jnp.float32)
        for q in range(3 * s, 3 * s + 3):
            rows_q = slice(q * K, (q + 1) * K)
            pair = both[rows_q]
            own_grad = own_grad + pupil_a[rows_q] * pair[:, :LANES] + pupil_b[rows_q] * pair[:, LANES:]
        grad = grad + (scale * weights[s]) * own_grad
    spec_send[...] = (norm * grad).astype(jnp.bfloat16)

    spread = {}
    start_half = me - lax.rem(me, half)
    for step in range(1, half):
        spread[step] = pltpu.make_async_remote_copy(
            src_ref=spec_send, dst_ref=spec_land.at[step],
            send_sem=spec_ssem.at[step], recv_sem=spec_rsem.at[step],
            device_id={"src": start_half + lax.rem(me + step, half)},
        )
        spread[step].start()
    for s in range(local):
        sums[s : s + 1, :] = jnp.sum(residual * power[s], 0, keepdims=True)
    sums_copy = pltpu.make_async_remote_copy(
        src_ref=sums, dst_ref=sums_land, send_sem=sums_sem.at[0], recv_sem=sums_sem.at[1],
        device_id={"tile": other},
    )
    sums_copy.start()

    lines = dot(table("own_rows", 0, 2 * grid), twice)
    lines_high = lines.astype(jnp.bfloat16)
    lines_low = (lines - lines_high.astype(jnp.float32)).astype(jnp.bfloat16)
    def stack(value):
        return jnp.concatenate([value, -sign * pltpu.roll(value, K, 1)], 0).astype(jnp.bfloat16)

    summed = spec_send[...].astype(jnp.float32)
    for step in range(1, half):
        spread[step].wait_recv()
        summed = summed + spec_land[step].astype(jnp.float32)

    spec_half[...] = summed.astype(jnp.bfloat16)

    def half_copy(slot, where):
        return pltpu.make_async_remote_copy(
            src_ref=spec_half, dst_ref=half_land.at[slot],
            send_sem=edge_ssem.at[slot], recv_sem=edge_rsem.at[slot], device_id=where,
        )

    def at_rim(index, which):
        return jnp.where(which == 0, index >= n - edges, index < edges)

    to_twin = half_copy(0, {"src": twin, "tile": tile})
    to_twin.start()
    rims = [
        (at_rim(twin, other), half_copy(1, {"src": twin, "tile": other})),
        (at_rim(me, other), half_copy(2, {"src": me, "tile": other})),
    ]
    for condition, copy in rims:
        pl.when(condition)(copy.start)
    image_out[...] = dot(jnp.concatenate([lines_high, lines_low], 1), table("tall_late", 4 * K))

    writes = [
        pltpu.make_async_copy(source, to, out_sem.at[i])
        for i, (source, to) in enumerate(zip((image_out, grad_out, source_out), outputs))
    ]
    writes[0].start()

    row_back, amb_back = table("own_rows", 2 * grid), table("amb_back")
    col_fwd_t = table("wide_late", th + 4 * grid)
    sums_copy.wait()
    both_sums = jnp.sum(sums[...] + sums_land[...], 1, keepdims=True) / (2 * th * tw)
    for s in range(local):
        source_out[s] = both_sums[s, 0]
    writes[2].start()

    to_twin.wait_recv()
    summed = summed + half_land[0].astype(jnp.float32)
    rows = dot(row_back, stack(summed))

    @pl.when(at_rim(me, tile))
    def _():
        for _, copy in rims:
            copy.wait_recv()
        outer = half_land[1].astype(jnp.float32) + half_land[2].astype(jnp.float32)
        full = rows + dot(amb_back, stack(outer))
        grad_out[...] = GRAD_SCALE * dot(full.astype(jnp.bfloat16), col_fwd_t)

    @pl.when(jnp.logical_not(at_rim(me, tile)))
    def _():
        grad_out[...] = GRAD_SCALE * dot(rows.astype(jnp.bfloat16), col_fwd_t)

    writes[1].start()
    to_twin.wait_send()
    for condition, copy in rims:
        pl.when(condition)(copy.wait_send)
    for step in range(1, half):
        spread[step].wait_send()
    for step in range(1, n):
        guarded(lax.rem(me + step, n) < owners, scatter[step].wait_send)
        guarded(me < owners, gather[step].wait_send)
    for copy in writes:
        copy.wait()


def write_outputs(image, grad, source, image_out, grad_out, source_out, held, scalars, sem):
    ways = [
        (image, held.at[0], image_out.at[0]),
        (grad, held.at[1], grad_out.at[0]),
        (source, scalars, source_out),
    ]
    loads = [pltpu.make_async_copy(w[0], w[1], sem.at[0, i]) for i, w in enumerate(ways)]
    stores = [pltpu.make_async_copy(w[1], w[2], sem.at[1, i]) for i, w in enumerate(ways)]
    for load in loads:
        load.start()
    for load, store in zip(loads, stores):
        load.wait()
        store.start()
    for store in stores:
        store.wait()


def body(
    mask_values, target_image, jones_pupil, polar_states, source_weights, pupil_offsets, polar_ids
):
    th, tw = mask_values.shape
    n = lax.axis_size("src")
    assert lax.axis_size("tile") == 2 and n % 2 == 0
    local = source_weights.shape[0]
    share = th // n
    grid = 2 * K
    owners = min(n, grid // ROWS_16)
    block_rows = grid // owners
    assert owners * block_rows == grid
    edges = -(-AMB // share)
    named = dict(
        mask=mask_values,
        target=target_image,
        jones=jones_pupil.reshape((-1,) + jones_pupil.shape[-2:]),
        offsets=pupil_offsets.T,
        ids=polar_ids,
        weights=source_weights,
        polar=polar_states.transpose(1, 2, 0),
    )
    constants = tables(th, tw)
    order = ["mask", "col_fwd", *SCALARS, "jones", "wide_early", "row_amb", "row_inv", "target"]
    order += [name for name in constants if name not in order]
    arrays = []
    held = []
    for name in order:
        value = named[name] if name in named else jnp.asarray(constants[name])
        arrays.append(value)
        shape = value.shape
        if name == "amb_back":
            shape = (share,) + shape[2:]
        elif name == "row_amb":
            shape = shape[1:]
        elif name == "own_rows":
            shape = (share,) + shape[1:]
        held.append((pltpu.SMEM if name in SCALARS else pltpu.VMEM)(shape, value.dtype))
    f32, bf16 = jnp.float32, jnp.bfloat16
    sems = pltpu.SemaphoreType.DMA
    scratch = held + [
        pltpu.VMEM((AMB, tw), bf16),
        pltpu.VMEM((AMB, LANES), bf16),
        pltpu.VMEM((AMB, LANES), bf16),
        pltpu.VMEM((3 * local * K, LANES), f32),
        pltpu.VMEM((3 * local * K, LANES), f32),
        pltpu.VMEM((2 * grid, 3 * local * grid), f32),
        pltpu.VMEM((local, grid, grid), f32),
        pltpu.VMEM((grid, grid), f32),
        pltpu.VMEM((grid, grid), bf16),
        pltpu.VMEM((n, block_rows, grid), bf16),
        pltpu.VMEM((block_rows, grid), bf16),
        pltpu.VMEM((grid, grid), bf16),
        pltpu.VMEM((K, LANES), bf16),
        pltpu.VMEM((n // 2, K, LANES), bf16),
        pltpu.VMEM((K, LANES), bf16),
        pltpu.VMEM((3, K, LANES), bf16),
        pltpu.VMEM((local, LANES), f32),
        pltpu.VMEM((local, LANES), f32),
        sems((len(order) + 1,)),
        sems((2,)),
        sems((n,)),
        sems((n,)),
        sems((n,)),
        sems((n,)),
        sems((n // 2,)),
        sems((n // 2,)),
        sems((3,)),
        sems((3,)),
        sems((2,)),
        pltpu.VMEM((share, tw), f32),
        pltpu.VMEM((share, tw), f32),
        pltpu.SMEM((local,), f32),
        sems((3,)),
    ]
    sizes = (n, local, th, tw, share, owners, block_rows, edges, local * n)
    in_hbm = pl.BlockSpec(memory_space=pltpu.HBM)
    results = pl.pallas_call(
        functools.partial(kernel, tuple(order), sizes),
        out_shape=(
            jax.ShapeDtypeStruct((share, tw), f32),
            jax.ShapeDtypeStruct((share, tw), f32),
            jax.ShapeDtypeStruct((local,), f32),
        ),
        in_specs=[in_hbm] * len(arrays),
        out_specs=(in_hbm,) * 3,
        scratch_shapes=scratch,
        compiler_params=pltpu.CompilerParams(
            collective_id=0, has_side_effects=True, vmem_limit_bytes=VMEM_LIMIT
        ),
    )(*arrays)
    return pl.pallas_call(
        write_outputs,
        out_shape=(
            jax.ShapeDtypeStruct((1, share, tw), f32),
            jax.ShapeDtypeStruct((1, share, tw), f32),
            jax.ShapeDtypeStruct((local,), f32),
        ),
        in_specs=[in_hbm] * 3,
        out_specs=(in_hbm,) * 3,
        scratch_shapes=[pltpu.VMEM((2, share, tw), f32), pltpu.SMEM((local,), f32), sems((2, 3))],
        compiler_params=pltpu.CompilerParams(vmem_limit_bytes=VMEM_LIMIT),
    )(*results)


def solution(mesh):
    placed = (
        P(("parts", "tile"), None),
        P(("parts", "tile"), None),
        P(),
        P(),
        P(("parts", "src")),
        P(("parts", "src"), None),
        P(("parts", "src")),
    )
    return jax.shard_map(
        body,
        mesh=mesh,
        in_specs=placed,
        out_specs=(
            P(("parts", "tile"), "src", None),
            P(("parts", "tile"), "src", None),
            P(("parts", "src")),
        ),
        check_vma=False,
    )
```

```python
import functools
import math

import jax
import jax.numpy as jnp
import ml_dtypes
import numpy as np
from jax import lax
from jax.experimental import pallas as pl
from jax.experimental.pallas import tpu as pltpu
from jax.sharding import PartitionSpec as P

AMB = 64
K = 64
GRAD_SCALE = 32.0
LANES = 2 * K
VMEM_LIMIT = 64 * 1024 * 1024 - 512 * 1024
ROWS_16 = 16


def split_bf16(table):
    high = table.astype(ml_dtypes.bfloat16)
    low = (table - high.astype(np.float64)).astype(ml_dtypes.bfloat16)
    return high, low


def tables(th, tw):
    window = th + 2 * AMB
    grid = 2 * K
    orders = np.arange(K) - K // 2
    diffs = np.arange(-(K - 1), K)

    def angle(left, right, period):
        return 2.0 * np.pi * np.mod(np.outer(left, right), period) / period

    bf = lambda x: np.ascontiguousarray(x).astype(ml_dtypes.bfloat16)
    col = angle(np.arange(tw), orders, tw)
    col_fwd = np.concatenate([np.cos(col), -np.sin(col)], 1)
    row = angle(orders, np.arange(window), window)
    row_fwd = np.concatenate([np.cos(row), np.sin(row)], 0)
    row_amb = np.stack([row_fwd[:, th + AMB :], row_fwd[:, :AMB]])
    row_back = row_fwd[:, AMB : AMB + th].T
    amb_back = np.zeros((2, th, 2 * K))
    amb_back[0, th - AMB :] = row_fwd[:, :AMB].T
    amb_back[1, :AMB] = row_fwd[:, th + AMB :].T
    small = angle(np.arange(grid), orders, grid)
    cos, sin = np.cos(small), np.sin(small)
    row_inv = np.concatenate(
        [np.concatenate([cos, -sin], 1), np.concatenate([sin, cos], 1)], 0
    )
    col_inv = np.concatenate(
        [np.concatenate([cos.T, sin.T], 1), np.concatenate([-sin.T, cos.T], 1)], 0
    )
    back = col_inv.T
    col_back = np.concatenate([back, back[:, K:], -back[:, :K]], 1)

    def dirichlet(positions):
        turn = positions[:, None] - np.arange(grid)[None, :] / grid
        return np.cos(2.0 * np.pi * turn[:, :, None] * diffs).sum(-1) / grid

    d_row = dirichlet((np.arange(th) + AMB) / window)
    d_col = dirichlet(np.arange(tw) / tw)
    gram = (tw / grid) * (d_row.T @ d_row)
    cat = lambda *parts: np.concatenate(parts, 1)
    wide_early = cat(bf(row_fwd[:, AMB : AMB + th]), bf(col_inv / K))
    wide_late = cat(bf(d_row.T), *split_bf16(gram), bf(row_inv.T), bf(col_fwd.T))
    tall_late = cat(bf(col_back), bf(np.concatenate([d_col.T, d_col.T], 0)))
    own_rows = cat(*split_bf16(d_row), bf(row_back))
    return dict(
        col_fwd=bf(col_fwd),
        wide_early=wide_early,
        row_amb=bf(row_amb),
        row_inv=bf(row_inv),
        d_col_t=bf(d_col),
        wide_late=wide_late,
        tall_late=tall_late,
        own_rows=own_rows,
        amb_back=bf(amb_back),
    )


SCALARS = ("offsets", "ids", "weights", "polar")
FIRST = ("rim", "col_fwd", "mask")


def dot(a, b):
    return jnp.dot(a, b, preferred_element_type=jnp.float32)


def kernel(names, sizes, *refs):
    n, local, th, tw, share, edges, parts_total = sizes
    grid = 2 * K
    count = len(names)
    hbm = dict(zip(names, refs[:count]))
    outputs = refs[count : 3 + count]
    vmem = dict(zip(names, refs[3 + count : 3 + 2 * count]))
    offsets, ids, weights, polar = (vmem[name] for name in SCALARS)
    (
        rim_rows, rim_send, halo, pupil_a, pupil_b, field, power, target_small,
        part, landed, spec_send, spec_land, edge_land, sums, sums_land,
        load_sem, halo_sem, gather_send, gather_recv,
        spec_ssem, spec_rsem, edge_ssem, edge_rsem, sums_sem,
        image_out, grad_out, source_out, out_sem,
    ) = refs[3 + 2 * count :]
    me = lax.axis_index("src")
    tile = lax.axis_index("tile")
    other = 1 - tile

    own = pl.ds(pl.multiple_of(me * share, share), share)
    rim = pl.ds(pl.multiple_of(other * (th - AMB), ROWS_16), AMB)
    parts_of = {
        "rim": lambda ref: ref.at[rim],
        "amb_back": lambda ref: ref.at[tile, own],
        "row_amb": lambda ref: ref.at[tile],
        "own_rows": lambda ref: ref.at[own],
    }
    loads = {}

    def load(chosen):
        for name in chosen:
            source = hbm["mask" if name == "rim" else name]
            source = parts_of[name](source) if name in parts_of else source
            target = rim_rows if name == "rim" else vmem[name]
            loads[name] = pltpu.make_async_copy(source, target, load_sem.at[len(loads)])
            loads[name].start()

    load(FIRST)
    barrier = pltpu.get_barrier_semaphore()
    for step in range(n):
        peer = lax.rem(me + step, n)
        if step:
            pl.semaphore_signal(barrier, inc=1, device_id={"src": peer, "tile": tile})
        pl.semaphore_signal(barrier, inc=1, device_id={"src": peer, "tile": other})
    load([name for name in names if name not in FIRST])
    waited = set()

    def table(name, start=0, stop=None):
        if name not in waited:
            loads[name].wait()
            waited.add(name)
        return vmem[name][:, start:stop]

    loads["rim"].wait()
    rim_send[...] = dot(rim_rows[...], table("col_fwd")).astype(jnp.bfloat16)
    pl.semaphore_wait(barrier, 2 * n - 1)
    halo_copy = pltpu.make_async_remote_copy(
        src_ref=rim_send, dst_ref=halo, send_sem=halo_sem.at[0], recv_sem=halo_sem.at[1],
        device_id={"tile": other},
    )
    halo_copy.start()
    partial = dot(table("mask"), table("col_fwd")).astype(jnp.bfloat16)

    for name in SCALARS + ("jones",):
        loads[name].wait()
    jones = vmem["jones"]
    lane = lax.broadcasted_iota(jnp.int32, (K, LANES), 1)
    left = lane < K
    for s in range(local):
        first, second, state = offsets[0, s], offsets[1, s], ids[s]
        low = lax.rem(LANES - second, LANES)
        high = K - second
        vec = [[polar[c, i, state] for i in range(2)] for c in range(2)]
        for j in range(3):
            win = [
                [jones[(c * 3 + j) * 2 + i, pl.ds(first, K), :] for i in range(2)]
                for c in range(2)
            ]
            real = sum(win[0][i] * vec[0][i] - win[1][i] * vec[1][i] for i in range(2))
            imag = sum(win[0][i] * vec[1][i] + win[1][i] * vec[0][i] for i in range(2))
            rows = slice((s * 3 + j) * K, (s * 3 + j + 1) * K)
            for value, kept in ((real, pupil_a), (imag, pupil_b)):
                kept[rows] = jnp.where(
                    left, pltpu.roll(value, low, 1), pltpu.roll(value, high, 1)
                )

    product = dot(table("wide_early", 0, th), partial)

    halo_copy.wait()
    product = product + dot(table("row_amb"), halo[...])
    sign = jnp.where(left, 1.0, -1.0)
    norm = 1.0 / math.sqrt((th + 2 * AMB) * tw)
    spec = norm * (product[:K] + sign * pltpu.roll(product[K:], K, 1))
    turned = -sign * pltpu.roll(spec, K, 1)

    fields = 3 * local
    masked = [
        pupil_a[q * K : (q + 1) * K] * spec + pupil_b[q * K : (q + 1) * K] * turned
        for q in range(fields)
    ]
    cols = dot(jnp.concatenate(masked, 0).astype(jnp.bfloat16), table("wide_early", th))
    cols = cols.astype(jnp.bfloat16)
    mixed = [
        jnp.concatenate([cols[q * K : (q + 1) * K, :grid], cols[q * K : (q + 1) * K, grid:]], 0)
        for q in range(fields)
    ]
    field[...] = dot(table("row_inv"), jnp.concatenate(mixed, 1))
    total = jnp.zeros((grid, grid), jnp.float32)
    for s in range(local):
        power_s = jnp.zeros((grid, grid), jnp.float32)
        for q in range(3 * s, 3 * s + 3):
            values = field[:, q * grid : (q + 1) * grid]
            power_s = power_s + values[:grid] * values[:grid] + values[grid:] * values[grid:]
        power[s] = power_s
        total = total + (weights[s] / parts_total) * power_s
    part[...] = total.astype(jnp.bfloat16)

    order = sorted(range(1, n), key=lambda step: -min(step, n - step))
    gather = {}
    for step in order:
        gather[step] = pltpu.make_async_remote_copy(
            src_ref=part, dst_ref=landed.at[step],
            send_sem=gather_send.at[step], recv_sem=gather_recv.at[step],
            device_id={"src": lax.rem(me + step, n)},
        )
        gather[step].start()

    projected = dot(table("target").astype(jnp.bfloat16), table("d_col_t")).astype(jnp.bfloat16)
    target_small[...] = dot(table("wide_late", 0, th), projected)

    row_inv_t = table("wide_late", th + 2 * grid, th + 4 * grid)
    col_back = table("tall_late", 0, 4 * K)
    gram = table("wide_late", th, th + 2 * grid)
    image = part[...].astype(jnp.float32)
    for step in reversed(order):
        gather[step].wait_recv()
        image = image + landed[step].astype(jnp.float32)
    image = image.astype(jnp.bfloat16)
    twice = jnp.concatenate([image, image], 0)
    residual = dot(gram, twice) - target_small[...]
    doubled = jnp.concatenate([residual, residual], 0)

    scaled = [
        (doubled * field[:, q * grid : (q + 1) * grid]).astype(jnp.bfloat16) for q in range(fields)
    ]
    rows = dot(row_inv_t, jnp.concatenate(scaled, 1)).astype(jnp.bfloat16)
    mixed = [
        jnp.concatenate([rows[:K, q * grid : (q + 1) * grid], rows[K:, q * grid : (q + 1) * grid]], 1)
        for q in range(fields)
    ]
    both = dot(jnp.concatenate(mixed, 0), col_back)
    grad = jnp.zeros((K, LANES), jnp.float32)
    scale = 2.0 / (parts_total * K)
    for s in range(local):
        own_grad = jnp.zeros((K, LANES), jnp.float32)
        for q in range(3 * s, 3 * s + 3):
            rows_q = slice(q * K, (q + 1) * K)
            pair = both[rows_q]
            own_grad = own_grad + pupil_a[rows_q] * pair[:, :LANES] + pupil_b[rows_q] * pair[:, LANES:]
        grad = grad + (scale * weights[s]) * own_grad
    spec_send[...] = (norm * grad).astype(jnp.bfloat16)

    spread, rims = {}, []
    for e in range(edges):
        rims.append(
            pltpu.make_async_remote_copy(
                src_ref=spec_send, dst_ref=edge_land.at[me],
                send_sem=edge_ssem.at[e], recv_sem=edge_rsem.at[me],
                device_id={"src": e + tile * (n - edges), "tile": other},
            )
        )
        rims[-1].start()
    for step in order:
        peer = lax.rem(me + step, n)
        spread[step] = pltpu.make_async_remote_copy(
            src_ref=spec_send, dst_ref=spec_land.at[step],
            send_sem=spec_ssem.at[step], recv_sem=spec_rsem.at[step],
            device_id={"src": peer},
        )
        spread[step].start()
    for s in range(local):
        sums[s : s + 1, :] = jnp.sum(residual * power[s], 0, keepdims=True)
    sums_copy = pltpu.make_async_remote_copy(
        src_ref=sums, dst_ref=sums_land, send_sem=sums_sem.at[0], recv_sem=sums_sem.at[1],
        device_id={"tile": other},
    )
    sums_copy.start()

    lines = dot(table("own_rows", 0, 2 * grid), twice)
    lines_high = lines.astype(jnp.bfloat16)
    lines_low = (lines - lines_high.astype(jnp.float32)).astype(jnp.bfloat16)
    image_out[...] = dot(jnp.concatenate([lines_high, lines_low], 1), table("tall_late", 4 * K))

    writes = [
        pltpu.make_async_copy(source, to, out_sem.at[i])
        for i, (source, to) in enumerate(zip((image_out, grad_out, source_out), outputs))
    ]
    writes[0].start()

    row_back, amb_back = table("own_rows", 2 * grid), table("amb_back")
    col_fwd_t = table("wide_late", th + 4 * grid)
    sums_copy.wait()
    both_sums = jnp.sum(sums[...] + sums_land[...], 1, keepdims=True) / (2 * th * tw)
    for s in range(local):
        source_out[s] = both_sums[s, 0]
    writes[2].start()

    def stack(value):
        return jnp.concatenate([value, -sign * pltpu.roll(value, K, 1)], 0).astype(jnp.bfloat16)

    summed = spec_send[...].astype(jnp.float32)
    for step in reversed(order):
        spread[step].wait_recv()
        summed = summed + spec_land[step].astype(jnp.float32)
    rows = dot(row_back, stack(summed))
    at_rim = jnp.where(tile == 0, me >= n - edges, me < edges)

    @pl.when(at_rim)
    def _():
        outer = jnp.zeros((K, LANES), jnp.float32)
        for d in range(n):
            pltpu.make_async_remote_copy(
                src_ref=spec_send, dst_ref=edge_land.at[d],
                send_sem=edge_ssem.at[0], recv_sem=edge_rsem.at[d],
                device_id={"tile": other},
            ).wait_recv()
            outer = outer + edge_land[d].astype(jnp.float32)
        full = rows + dot(amb_back, stack(outer))
        grad_out[...] = GRAD_SCALE * dot(full.astype(jnp.bfloat16), col_fwd_t)

    @pl.when(jnp.logical_not(at_rim))
    def _():
        grad_out[...] = GRAD_SCALE * dot(rows.astype(jnp.bfloat16), col_fwd_t)

    writes[1].start()
    for step in range(1, n):
        gather[step].wait_send()
        spread[step].wait_send()
    for copy in rims:
        copy.wait_send()
    for copy in writes:
        copy.wait()


def write_outputs(image, grad, source, image_out, grad_out, source_out, held, scalars, sem):
    ways = [
        (image, held.at[0], image_out.at[0]),
        (grad, held.at[1], grad_out.at[0]),
        (source, scalars, source_out),
    ]
    loads = [pltpu.make_async_copy(w[0], w[1], sem.at[0, i]) for i, w in enumerate(ways)]
    stores = [pltpu.make_async_copy(w[1], w[2], sem.at[1, i]) for i, w in enumerate(ways)]
    for load in loads:
        load.start()
    for load, store in zip(loads, stores):
        load.wait()
        store.start()
    for store in stores:
        store.wait()


def body(
    mask_values, target_image, jones_pupil, polar_states, source_weights, pupil_offsets, polar_ids
):
    th, tw = mask_values.shape
    n = lax.axis_size("src")
    assert lax.axis_size("tile") == 2
    local = source_weights.shape[0]
    share = th // n
    grid = 2 * K
    edges = -(-AMB // share)
    named = dict(
        mask=mask_values,
        target=target_image,
        jones=jones_pupil.reshape((-1,) + jones_pupil.shape[-2:]),
        offsets=pupil_offsets.T,
        ids=polar_ids,
        weights=source_weights,
        polar=polar_states.transpose(1, 2, 0),
    )
    constants = tables(th, tw)
    order = ["mask", "col_fwd", *SCALARS, "jones", "wide_early", "row_amb", "row_inv", "target"]
    order += [name for name in constants if name not in order]
    arrays = []
    held = []
    for name in order:
        value = named[name] if name in named else jnp.asarray(constants[name])
        arrays.append(value)
        shape = value.shape
        if name == "amb_back":
            shape = (share,) + shape[2:]
        elif name == "row_amb":
            shape = shape[1:]
        elif name == "own_rows":
            shape = (share,) + shape[1:]
        held.append((pltpu.SMEM if name in SCALARS else pltpu.VMEM)(shape, value.dtype))
    f32, bf16 = jnp.float32, jnp.bfloat16
    sems = pltpu.SemaphoreType.DMA
    scratch = held + [
        pltpu.VMEM((AMB, tw), bf16),
        pltpu.VMEM((AMB, LANES), bf16),
        pltpu.VMEM((AMB, LANES), bf16),
        pltpu.VMEM((3 * local * K, LANES), f32),
        pltpu.VMEM((3 * local * K, LANES), f32),
        pltpu.VMEM((2 * grid, 3 * local * grid), f32),
        pltpu.VMEM((local, grid, grid), f32),
        pltpu.VMEM((grid, grid), f32),
        pltpu.VMEM((grid, grid), bf16),
        pltpu.VMEM((n, grid, grid), bf16),
        pltpu.VMEM((K, LANES), bf16),
        pltpu.VMEM((n, K, LANES), bf16),
        pltpu.VMEM((n, K, LANES), bf16),
        pltpu.VMEM((local, LANES), f32),
        pltpu.VMEM((local, LANES), f32),
        sems((len(order) + 1,)),
        sems((2,)),
        sems((n,)),
        sems((n,)),
        sems((n,)),
        sems((n,)),
        sems((edges,)),
        sems((n,)),
        sems((2,)),
        pltpu.VMEM((share, tw), f32),
        pltpu.VMEM((share, tw), f32),
        pltpu.SMEM((local,), f32),
        sems((3,)),
    ]
    sizes = (n, local, th, tw, share, edges, local * n)
    in_hbm = pl.BlockSpec(memory_space=pltpu.HBM)
    results = pl.pallas_call(
        functools.partial(kernel, tuple(order), sizes),
        out_shape=(
            jax.ShapeDtypeStruct((share, tw), f32),
            jax.ShapeDtypeStruct((share, tw), f32),
            jax.ShapeDtypeStruct((local,), f32),
        ),
        in_specs=[in_hbm] * len(arrays),
        out_specs=(in_hbm,) * 3,
        scratch_shapes=scratch,
        compiler_params=pltpu.CompilerParams(
            collective_id=0, has_side_effects=True, vmem_limit_bytes=VMEM_LIMIT
        ),
    )(*arrays)
    return pl.pallas_call(
        write_outputs,
        out_shape=(
            jax.ShapeDtypeStruct((1, share, tw), f32),
            jax.ShapeDtypeStruct((1, share, tw), f32),
            jax.ShapeDtypeStruct((local,), f32),
        ),
        in_specs=[in_hbm] * 3,
        out_specs=(in_hbm,) * 3,
        scratch_shapes=[pltpu.VMEM((2, share, tw), f32), pltpu.SMEM((local,), f32), sems((2, 3))],
        compiler_params=pltpu.CompilerParams(vmem_limit_bytes=VMEM_LIMIT),
    )(*results)


def solution(mesh):
    placed = (
        P(("parts", "tile"), None),
        P(("parts", "tile"), None),
        P(),
        P(),
        P(("parts", "src")),
        P(("parts", "src"), None),
        P(("parts", "src")),
    )
    return jax.shard_map(
        body,
        mesh=mesh,
        in_specs=placed,
        out_specs=(
            P(("parts", "tile"), "src", None),
            P(("parts", "tile"), "src", None),
            P(("parts", "src")),
        ),
        check_vma=False,
    )
```

```python
import functools
import math

import jax
import jax.numpy as jnp
import ml_dtypes
import numpy as np
from jax import lax
from jax.experimental import pallas as pl
from jax.experimental.pallas import tpu as pltpu
from jax.sharding import PartitionSpec as P

AMB = 64
K = 64
GRAD_SCALE = 32.0
LANES = 2 * K
VMEM_LIMIT = 64 * 1024 * 1024 - 512 * 1024
ROWS_16 = 16


def split_bf16(table):
    high = table.astype(ml_dtypes.bfloat16)
    low = (table - high.astype(np.float64)).astype(ml_dtypes.bfloat16)
    return high, low


def tables(th, tw):
    window = th + 2 * AMB
    grid = 2 * K
    orders = np.arange(K) - K // 2
    diffs = np.arange(-(K - 1), K)

    def angle(left, right, period):
        return 2.0 * np.pi * np.mod(np.outer(left, right), period) / period

    bf = lambda x: np.ascontiguousarray(x).astype(ml_dtypes.bfloat16)
    col = angle(np.arange(tw), orders, tw)
    col_fwd = np.concatenate([np.cos(col), -np.sin(col)], 1)
    row = angle(orders, np.arange(window), window)
    row_fwd = np.concatenate([np.cos(row), np.sin(row)], 0)
    row_amb = np.stack([row_fwd[:, th + AMB :], row_fwd[:, :AMB]])
    row_back = row_fwd[:, AMB : AMB + th].T
    amb_back = np.zeros((2, th, 2 * K))
    amb_back[0, th - AMB :] = row_fwd[:, :AMB].T
    amb_back[1, :AMB] = row_fwd[:, th + AMB :].T
    small = angle(np.arange(grid), orders, grid)
    cos, sin = np.cos(small), np.sin(small)
    row_inv = np.concatenate(
        [np.concatenate([cos, -sin], 1), np.concatenate([sin, cos], 1)], 0
    )
    col_inv = np.concatenate(
        [np.concatenate([cos.T, sin.T], 1), np.concatenate([-sin.T, cos.T], 1)], 0
    )
    back = col_inv.T
    col_back = np.concatenate([back, back[:, K:], -back[:, :K]], 1)

    def dirichlet(positions):
        turn = positions[:, None] - np.arange(grid)[None, :] / grid
        return np.cos(2.0 * np.pi * turn[:, :, None] * diffs).sum(-1) / grid

    d_row = dirichlet((np.arange(th) + AMB) / window)
    d_col = dirichlet(np.arange(tw) / tw)
    gram = (tw / grid) * (d_row.T @ d_row)
    cat = lambda *parts: np.concatenate(parts, 1)
    wide_early = cat(bf(row_fwd[:, AMB : AMB + th]), bf(col_inv / K))
    wide_late = cat(bf(d_row.T), *split_bf16(gram), bf(row_inv.T), bf(col_fwd.T))
    tall_late = cat(bf(col_back), bf(np.concatenate([d_col.T, d_col.T], 0)))
    own_rows = cat(*split_bf16(d_row), bf(row_back))
    return dict(
        col_fwd=bf(col_fwd),
        wide_early=wide_early,
        row_amb=bf(row_amb),
        row_inv=bf(row_inv),
        d_col_t=bf(d_col),
        wide_late=wide_late,
        tall_late=tall_late,
        own_rows=own_rows,
        amb_back=bf(amb_back),
    )


SCALARS = ("offsets", "ids", "weights", "polar")
FIRST = ("rim", "col_fwd", "mask")


def dot(a, b):
    return jnp.dot(a, b, preferred_element_type=jnp.float32)


def kernel(names, sizes, *refs):
    n, local, th, tw, share, owners, block_rows, edges, parts_total = sizes
    grid = 2 * K
    count = len(names)
    hbm = dict(zip(names, refs[:count]))
    outputs = refs[count : 3 + count]
    vmem = dict(zip(names, refs[3 + count : 3 + 2 * count]))
    offsets, ids, weights, polar = (vmem[name] for name in SCALARS)
    (
        rim_rows, rim_send, halo, pupil_a, pupil_b, field, power, target_small,
        part, landed, reduced, whole, spec_send, spec_land, edge_land, sums, sums_land,
        load_sem, halo_sem, scatter_send, scatter_recv, gather_send, gather_recv,
        spec_ssem, spec_rsem, edge_ssem, edge_rsem, sums_sem,
        image_out, grad_out, source_out, out_sem,
    ) = refs[3 + 2 * count :]
    me = lax.axis_index("src")
    tile = lax.axis_index("tile")
    other = 1 - tile

    own = pl.ds(pl.multiple_of(me * share, share), share)
    rim = pl.ds(pl.multiple_of(other * (th - AMB), ROWS_16), AMB)
    parts_of = {
        "rim": lambda ref: ref.at[rim],
        "amb_back": lambda ref: ref.at[tile, own],
        "row_amb": lambda ref: ref.at[tile],
        "own_rows": lambda ref: ref.at[own],
    }
    loads = {}

    def load(chosen):
        for name in chosen:
            source = hbm["mask" if name == "rim" else name]
            source = parts_of[name](source) if name in parts_of else source
            target = rim_rows if name == "rim" else vmem[name]
            loads[name] = pltpu.make_async_copy(source, target, load_sem.at[len(loads)])
            loads[name].start()

    order = sorted(range(1, n), key=lambda step: -min(step, n - step))
    barrier = pltpu.get_barrier_semaphore()
    pl.semaphore_signal(barrier, inc=1, device_id={"tile": other})
    load(FIRST)
    for step in order:
        peer = lax.rem(me + step, n)
        for which in (tile, other):
            pl.semaphore_signal(barrier, inc=1, device_id={"src": peer, "tile": which})
    load([name for name in names if name not in FIRST])
    waited = set()

    def table(name, start=0, stop=None):
        if name not in waited:
            loads[name].wait()
            waited.add(name)
        return vmem[name][:, start:stop]

    loads["rim"].wait()
    rim_send[...] = dot(rim_rows[...], table("col_fwd")).astype(jnp.bfloat16)
    pl.semaphore_wait(barrier, 2 * n - 1)
    halo_copy = pltpu.make_async_remote_copy(
        src_ref=rim_send, dst_ref=halo, send_sem=halo_sem.at[0], recv_sem=halo_sem.at[1],
        device_id={"tile": other},
    )
    halo_copy.start()
    partial = dot(table("mask"), table("col_fwd")).astype(jnp.bfloat16)

    for name in SCALARS + ("jones",):
        loads[name].wait()
    jones = vmem["jones"]
    lane = lax.broadcasted_iota(jnp.int32, (K, LANES), 1)
    left = lane < K
    for s in range(local):
        first, second, state = offsets[0, s], offsets[1, s], ids[s]
        low = lax.rem(LANES - second, LANES)
        high = K - second
        vec = [[polar[c, i, state] for i in range(2)] for c in range(2)]
        for j in range(3):
            win = [
                [jones[(c * 3 + j) * 2 + i, pl.ds(first, K), :] for i in range(2)]
                for c in range(2)
            ]
            real = sum(win[0][i] * vec[0][i] - win[1][i] * vec[1][i] for i in range(2))
            imag = sum(win[0][i] * vec[1][i] + win[1][i] * vec[0][i] for i in range(2))
            rows = slice((s * 3 + j) * K, (s * 3 + j + 1) * K)
            for value, kept in ((real, pupil_a), (imag, pupil_b)):
                kept[rows] = jnp.where(
                    left, pltpu.roll(value, low, 1), pltpu.roll(value, high, 1)
                )

    product = dot(table("wide_early", 0, th), partial)

    halo_copy.wait()
    product = product + dot(table("row_amb"), halo[...])
    sign = jnp.where(left, 1.0, -1.0)
    norm = 1.0 / math.sqrt((th + 2 * AMB) * tw)
    spec = norm * (product[:K] + sign * pltpu.roll(product[K:], K, 1))
    turned = -sign * pltpu.roll(spec, K, 1)

    fields = 3 * local
    masked = [
        pupil_a[q * K : (q + 1) * K] * spec + pupil_b[q * K : (q + 1) * K] * turned
        for q in range(fields)
    ]
    cols = dot(jnp.concatenate(masked, 0).astype(jnp.bfloat16), table("wide_early", th))
    cols = cols.astype(jnp.bfloat16)
    mixed = [
        jnp.concatenate([cols[q * K : (q + 1) * K, :grid], cols[q * K : (q + 1) * K, grid:]], 0)
        for q in range(fields)
    ]
    field[...] = dot(table("row_inv"), jnp.concatenate(mixed, 1))
    total = jnp.zeros((grid, grid), jnp.float32)
    for s in range(local):
        power_s = jnp.zeros((grid, grid), jnp.float32)
        for q in range(3 * s, 3 * s + 3):
            values = field[:, q * grid : (q + 1) * grid]
            power_s = power_s + values[:grid] * values[:grid] + values[grid:] * values[grid:]
        power[s] = power_s
        total = total + (weights[s] / parts_total) * power_s
    part[...] = total.astype(jnp.bfloat16)

    def block(index):
        return pl.ds(pl.multiple_of(index * block_rows, block_rows), block_rows)

    def guarded(condition, run):
        if owners == n:
            run()
        else:
            pl.when(condition)(run)

    scatter, gather = {}, {}
    for step in order:
        peer = lax.rem(me + step, n)
        to = peer if owners == n else jnp.minimum(peer, owners - 1)
        scatter[step] = pltpu.make_async_remote_copy(
            src_ref=part.at[block(to)], dst_ref=landed.at[step],
            send_sem=scatter_send.at[step], recv_sem=scatter_recv.at[step],
            device_id={"src": peer},
        )
        guarded(peer < owners, scatter[step].start)
    mine = me if owners == n else jnp.minimum(me, owners - 1)

    def reduce_own():
        acc = part[block(mine), :].astype(jnp.float32)
        for step in reversed(order):
            scatter[step].wait_recv()
            acc = acc + landed[step].astype(jnp.float32)
        reduced[...] = acc.astype(jnp.bfloat16)
        for step in order:
            gather[step].start()
        whole[block(mine), :] = reduced[...]

    for step in range(1, n):
        peer = lax.rem(me + step, n)
        gather[step] = pltpu.make_async_remote_copy(
            src_ref=reduced, dst_ref=whole.at[block(mine)],
            send_sem=gather_send.at[step], recv_sem=gather_recv.at[step],
            device_id={"src": peer},
        )
    projected = dot(table("target").astype(jnp.bfloat16), table("d_col_t")).astype(jnp.bfloat16)
    target_small[...] = dot(table("wide_late", 0, th), projected)

    guarded(me < owners, reduce_own)
    row_inv_t = table("wide_late", th + 2 * grid, th + 4 * grid)
    col_back = table("tall_late", 0, 4 * K)
    gram = table("wide_late", th, th + 2 * grid)
    for step in reversed(order):
        origin = lax.rem(me + n - step, n)
        guarded(origin < owners, gather[step].wait_recv)

    image = whole[...]
    twice = jnp.concatenate([image, image], 0)
    residual = dot(gram, twice) - target_small[...]
    doubled = jnp.concatenate([residual, residual], 0)

    scaled = [
        (doubled * field[:, q * grid : (q + 1) * grid]).astype(jnp.bfloat16) for q in range(fields)
    ]
    rows = dot(row_inv_t, jnp.concatenate(scaled, 1)).astype(jnp.bfloat16)
    mixed = [
        jnp.concatenate([rows[:K, q * grid : (q + 1) * grid], rows[K:, q * grid : (q + 1) * grid]], 1)
        for q in range(fields)
    ]
    both = dot(jnp.concatenate(mixed, 0), col_back)
    grad = jnp.zeros((K, LANES), jnp.float32)
    scale = 2.0 / (parts_total * K)
    for s in range(local):
        own_grad = jnp.zeros((K, LANES), jnp.float32)
        for q in range(3 * s, 3 * s + 3):
            rows_q = slice(q * K, (q + 1) * K)
            pair = both[rows_q]
            own_grad = own_grad + pupil_a[rows_q] * pair[:, :LANES] + pupil_b[rows_q] * pair[:, LANES:]
        grad = grad + (scale * weights[s]) * own_grad
    spec_send[...] = (norm * grad).astype(jnp.bfloat16)

    spread, rims = {}, []
    for e in range(edges):
        rims.append(
            pltpu.make_async_remote_copy(
                src_ref=spec_send, dst_ref=edge_land.at[me],
                send_sem=edge_ssem.at[e], recv_sem=edge_rsem.at[me],
                device_id={"src": e + tile * (n - edges), "tile": other},
            )
        )
        rims[-1].start()
    for step in order:
        peer = lax.rem(me + step, n)
        spread[step] = pltpu.make_async_remote_copy(
            src_ref=spec_send, dst_ref=spec_land.at[step],
            send_sem=spec_ssem.at[step], recv_sem=spec_rsem.at[step],
            device_id={"src": peer},
        )
        spread[step].start()
    for s in range(local):
        sums[s : s + 1, :] = jnp.sum(residual * power[s], 0, keepdims=True)
    sums_copy = pltpu.make_async_remote_copy(
        src_ref=sums, dst_ref=sums_land, send_sem=sums_sem.at[0], recv_sem=sums_sem.at[1],
        device_id={"tile": other},
    )
    sums_copy.start()

    lines = dot(table("own_rows", 0, 2 * grid), twice)
    lines_high = lines.astype(jnp.bfloat16)
    lines_low = (lines - lines_high.astype(jnp.float32)).astype(jnp.bfloat16)
    image_out[...] = dot(jnp.concatenate([lines_high, lines_low], 1), table("tall_late", 4 * K))

    writes = [
        pltpu.make_async_copy(source, to, out_sem.at[i])
        for i, (source, to) in enumerate(zip((image_out, grad_out, source_out), outputs))
    ]
    writes[0].start()

    row_back, amb_back = table("own_rows", 2 * grid), table("amb_back")
    col_fwd_t = table("wide_late", th + 4 * grid)
    sums_copy.wait()
    both_sums = jnp.sum(sums[...] + sums_land[...], 1, keepdims=True) / (2 * th * tw)
    for s in range(local):
        source_out[s] = both_sums[s, 0]
    writes[2].start()

    def stack(value):
        return jnp.concatenate([value, -sign * pltpu.roll(value, K, 1)], 0).astype(jnp.bfloat16)

    summed = spec_send[...].astype(jnp.float32)
    for step in reversed(order):
        spread[step].wait_recv()
        summed = summed + spec_land[step].astype(jnp.float32)
    rows = dot(row_back, stack(summed))
    at_rim = jnp.where(tile == 0, me >= n - edges, me < edges)

    @pl.when(at_rim)
    def _():
        outer = jnp.zeros((K, LANES), jnp.float32)
        for d in range(n):
            pltpu.make_async_remote_copy(
                src_ref=spec_send, dst_ref=edge_land.at[d],
                send_sem=edge_ssem.at[0], recv_sem=edge_rsem.at[d],
                device_id={"tile": other},
            ).wait_recv()
            outer = outer + edge_land[d].astype(jnp.float32)
        full = rows + dot(amb_back, stack(outer))
        grad_out[...] = GRAD_SCALE * dot(full.astype(jnp.bfloat16), col_fwd_t)

    @pl.when(jnp.logical_not(at_rim))
    def _():
        grad_out[...] = GRAD_SCALE * dot(rows.astype(jnp.bfloat16), col_fwd_t)

    writes[1].start()
    for step in range(1, n):
        guarded(lax.rem(me + step, n) < owners, scatter[step].wait_send)
        guarded(me < owners, gather[step].wait_send)
        spread[step].wait_send()
    for copy in rims:
        copy.wait_send()
    for copy in writes:
        copy.wait()


def write_outputs(image, grad, source, image_out, grad_out, source_out, held, scalars, sem):
    ways = [
        (image, held.at[0], image_out.at[0]),
        (grad, held.at[1], grad_out.at[0]),
        (source, scalars, source_out),
    ]
    loads = [pltpu.make_async_copy(w[0], w[1], sem.at[0, i]) for i, w in enumerate(ways)]
    stores = [pltpu.make_async_copy(w[1], w[2], sem.at[1, i]) for i, w in enumerate(ways)]
    for load in loads:
        load.start()
    for load, store in zip(loads, stores):
        load.wait()
        store.start()
    for store in stores:
        store.wait()


def body(
    mask_values, target_image, jones_pupil, polar_states, source_weights, pupil_offsets, polar_ids
):
    th, tw = mask_values.shape
    n = lax.axis_size("src")
    assert lax.axis_size("tile") == 2
    local = source_weights.shape[0]
    share = th // n
    grid = 2 * K
    owners = min(n, grid // ROWS_16)
    block_rows = grid // owners
    assert owners * block_rows == grid
    edges = -(-AMB // share)
    named = dict(
        mask=mask_values,
        target=target_image,
        jones=jones_pupil.reshape((-1,) + jones_pupil.shape[-2:]),
        offsets=pupil_offsets.T,
        ids=polar_ids,
        weights=source_weights,
        polar=polar_states.transpose(1, 2, 0),
    )
    constants = tables(th, tw)
    order = ["mask", "col_fwd", *SCALARS, "jones", "wide_early", "row_amb", "row_inv", "target"]
    order += [name for name in constants if name not in order]
    arrays = []
    held = []
    for name in order:
        value = named[name] if name in named else jnp.asarray(constants[name])
        arrays.append(value)
        shape = value.shape
        if name == "amb_back":
            shape = (share,) + shape[2:]
        elif name == "row_amb":
            shape = shape[1:]
        elif name == "own_rows":
            shape = (share,) + shape[1:]
        held.append((pltpu.SMEM if name in SCALARS else pltpu.VMEM)(shape, value.dtype))
    f32, bf16 = jnp.float32, jnp.bfloat16
    sems = pltpu.SemaphoreType.DMA
    scratch = held + [
        pltpu.VMEM((AMB, tw), bf16),
        pltpu.VMEM((AMB, LANES), bf16),
        pltpu.VMEM((AMB, LANES), bf16),
        pltpu.VMEM((3 * local * K, LANES), f32),
        pltpu.VMEM((3 * local * K, LANES), f32),
        pltpu.VMEM((2 * grid, 3 * local * grid), f32),
        pltpu.VMEM((local, grid, grid), f32),
        pltpu.VMEM((grid, grid), f32),
        pltpu.VMEM((grid, grid), bf16),
        pltpu.VMEM((n, block_rows, grid), bf16),
        pltpu.VMEM((block_rows, grid), bf16),
        pltpu.VMEM((grid, grid), bf16),
        pltpu.VMEM((K, LANES), bf16),
        pltpu.VMEM((n, K, LANES), bf16),
        pltpu.VMEM((n, K, LANES), bf16),
        pltpu.VMEM((local, LANES), f32),
        pltpu.VMEM((local, LANES), f32),
        sems((len(order) + 1,)),
        sems((2,)),
        sems((n,)),
        sems((n,)),
        sems((n,)),
        sems((n,)),
        sems((n,)),
        sems((n,)),
        sems((edges,)),
        sems((n,)),
        sems((2,)),
        pltpu.VMEM((share, tw), f32),
        pltpu.VMEM((share, tw), f32),
        pltpu.SMEM((local,), f32),
        sems((3,)),
    ]
    sizes = (n, local, th, tw, share, owners, block_rows, edges, local * n)
    in_hbm = pl.BlockSpec(memory_space=pltpu.HBM)
    results = pl.pallas_call(
        functools.partial(kernel, tuple(order), sizes),
        out_shape=(
            jax.ShapeDtypeStruct((share, tw), f32),
            jax.ShapeDtypeStruct((share, tw), f32),
            jax.ShapeDtypeStruct((local,), f32),
        ),
        in_specs=[in_hbm] * len(arrays),
        out_specs=(in_hbm,) * 3,
        scratch_shapes=scratch,
        compiler_params=pltpu.CompilerParams(
            collective_id=0, has_side_effects=True, vmem_limit_bytes=VMEM_LIMIT
        ),
    )(*arrays)
    return pl.pallas_call(
        write_outputs,
        out_shape=(
            jax.ShapeDtypeStruct((1, share, tw), f32),
            jax.ShapeDtypeStruct((1, share, tw), f32),
            jax.ShapeDtypeStruct((local,), f32),
        ),
        in_specs=[in_hbm] * 3,
        out_specs=(in_hbm,) * 3,
        scratch_shapes=[pltpu.VMEM((2, share, tw), f32), pltpu.SMEM((local,), f32), sems((2, 3))],
        compiler_params=pltpu.CompilerParams(vmem_limit_bytes=VMEM_LIMIT),
    )(*results)


def solution(mesh):
    placed = (
        P(("parts", "tile"), None),
        P(("parts", "tile"), None),
        P(),
        P(),
        P(("parts", "src")),
        P(("parts", "src"), None),
        P(("parts", "src")),
    )
    return jax.shard_map(
        body,
        mesh=mesh,
        in_specs=placed,
        out_specs=(
            P(("parts", "tile"), "src", None),
            P(("parts", "tile"), "src", None),
            P(("parts", "src")),
        ),
        check_vma=False,
    )
```

```python
import functools
import math

import jax
import jax.numpy as jnp
import ml_dtypes
import numpy as np
from jax import lax
from jax.experimental import pallas as pl
from jax.experimental.pallas import tpu as pltpu
from jax.sharding import PartitionSpec as P

AMB = 64
K = 64
GRAD_SCALE = 32.0
LANES = 2 * K
VMEM_LIMIT = 64 * 1024 * 1024 - 512 * 1024
ROWS_16 = 16


def split_bf16(table):
    high = table.astype(ml_dtypes.bfloat16)
    low = (table - high.astype(np.float64)).astype(ml_dtypes.bfloat16)
    return high, low


def tables(th, tw):
    window = th + 2 * AMB
    grid = 2 * K
    orders = np.arange(K) - K // 2
    diffs = np.arange(-(K - 1), K)

    def angle(left, right, period):
        return 2.0 * np.pi * np.mod(np.outer(left, right), period) / period

    bf = lambda x: np.ascontiguousarray(x).astype(ml_dtypes.bfloat16)
    col = angle(np.arange(tw), orders, tw)
    col_fwd = np.concatenate([np.cos(col), -np.sin(col)], 1)
    row = angle(orders, np.arange(window), window)
    row_fwd = np.concatenate([np.cos(row), np.sin(row)], 0)
    row_amb = np.stack([row_fwd[:, th + AMB :], row_fwd[:, :AMB]])
    row_back = row_fwd[:, AMB : AMB + th].T
    amb_back = np.zeros((2, th, 2 * K))
    amb_back[0, th - AMB :] = row_fwd[:, :AMB].T
    amb_back[1, :AMB] = row_fwd[:, th + AMB :].T
    small = angle(np.arange(grid), orders, grid)
    cos, sin = np.cos(small), np.sin(small)
    row_inv = np.concatenate(
        [np.concatenate([cos, -sin], 1), np.concatenate([sin, cos], 1)], 0
    )
    col_inv = np.concatenate(
        [np.concatenate([cos.T, sin.T], 1), np.concatenate([-sin.T, cos.T], 1)], 0
    )
    back = col_inv.T
    col_back = np.concatenate([back, back[:, K:], -back[:, :K]], 1)

    def dirichlet(positions):
        turn = positions[:, None] - np.arange(grid)[None, :] / grid
        return np.cos(2.0 * np.pi * turn[:, :, None] * diffs).sum(-1) / grid

    d_row = dirichlet((np.arange(th) + AMB) / window)
    d_col = dirichlet(np.arange(tw) / tw)
    gram = (tw / grid) * (d_row.T @ d_row)
    cat = lambda *parts: np.concatenate(parts, 1)
    wide_early = cat(bf(row_fwd[:, AMB : AMB + th]), bf(col_inv / K))
    wide_late = cat(bf(d_row.T), *split_bf16(gram), bf(row_inv.T), bf(col_fwd.T))
    tall_late = cat(bf(col_back), bf(np.concatenate([d_col.T, d_col.T], 0)))
    own_rows = cat(*split_bf16(d_row), bf(row_back))
    return dict(
        col_fwd=bf(col_fwd),
        wide_early=wide_early,
        row_amb=bf(row_amb),
        row_inv=bf(row_inv),
        d_col_t=bf(d_col),
        wide_late=wide_late,
        tall_late=tall_late,
        own_rows=own_rows,
        amb_back=bf(amb_back),
    )


SCALARS = ("offsets", "ids", "weights", "polar")
FIRST = ("rim", "col_fwd", "mask")


def dot(a, b):
    return jnp.dot(a, b, preferred_element_type=jnp.float32)


def kernel(names, sizes, *refs):
    n, local, th, tw, share, owners, block_rows, edges, parts_total = sizes
    grid = 2 * K
    count = len(names)
    hbm = dict(zip(names, refs[:count]))
    outputs = refs[count : 3 + count]
    vmem = dict(zip(names, refs[3 + count : 3 + 2 * count]))
    offsets, ids, weights, polar = (vmem[name] for name in SCALARS)
    (
        rim_rows, rim_send, halo, pupil_a, pupil_b, field, power, target_small,
        part, landed, reduced, whole, spec_send, spec_land, edge_land, sums, sums_land,
        load_sem, halo_sem, scatter_send, scatter_recv, gather_send, gather_recv,
        spec_ssem, spec_rsem, edge_ssem, edge_rsem, sums_sem,
        image_out, grad_out, source_out, out_sem,
    ) = refs[3 + 2 * count :]
    me = lax.axis_index("src")
    tile = lax.axis_index("tile")
    other = 1 - tile

    own = pl.ds(pl.multiple_of(me * share, share), share)
    rim = pl.ds(pl.multiple_of(other * (th - AMB), ROWS_16), AMB)
    parts_of = {
        "rim": lambda ref: ref.at[rim],
        "amb_back": lambda ref: ref.at[tile, own],
        "row_amb": lambda ref: ref.at[tile],
        "own_rows": lambda ref: ref.at[own],
    }
    loads = {}

    def load(chosen):
        for name in chosen:
            source = hbm["mask" if name == "rim" else name]
            source = parts_of[name](source) if name in parts_of else source
            target = rim_rows if name == "rim" else vmem[name]
            loads[name] = pltpu.make_async_copy(source, target, load_sem.at[len(loads)])
            loads[name].start()

    load(FIRST)
    barrier = pltpu.get_barrier_semaphore()
    for step in range(n):
        peer = lax.rem(me + step, n)
        if step:
            pl.semaphore_signal(barrier, inc=1, device_id={"src": peer, "tile": tile})
        pl.semaphore_signal(barrier, inc=1, device_id={"src": peer, "tile": other})
    load([name for name in names if name not in FIRST])
    waited = set()

    def table(name, start=0, stop=None):
        if name not in waited:
            loads[name].wait()
            waited.add(name)
        return vmem[name][:, start:stop]

    loads["rim"].wait()
    rim_send[...] = dot(rim_rows[...], table("col_fwd")).astype(jnp.bfloat16)
    pl.semaphore_wait(barrier, 2 * n - 1)
    halo_copy = pltpu.make_async_remote_copy(
        src_ref=rim_send, dst_ref=halo, send_sem=halo_sem.at[0], recv_sem=halo_sem.at[1],
        device_id={"tile": other},
    )
    halo_copy.start()
    partial = dot(table("mask"), table("col_fwd")).astype(jnp.bfloat16)

    for name in SCALARS + ("jones",):
        loads[name].wait()
    jones = vmem["jones"]
    lane = lax.broadcasted_iota(jnp.int32, (K, LANES), 1)
    left = lane < K
    for s in range(local):
        first, second, state = offsets[0, s], offsets[1, s], ids[s]
        low = lax.rem(LANES - second, LANES)
        high = K - second
        vec = [[polar[c, i, state] for i in range(2)] for c in range(2)]
        for j in range(3):
            win = [
                [jones[(c * 3 + j) * 2 + i, pl.ds(first, K), :] for i in range(2)]
                for c in range(2)
            ]
            real = sum(win[0][i] * vec[0][i] - win[1][i] * vec[1][i] for i in range(2))
            imag = sum(win[0][i] * vec[1][i] + win[1][i] * vec[0][i] for i in range(2))
            rows = slice((s * 3 + j) * K, (s * 3 + j + 1) * K)
            for value, kept in ((real, pupil_a), (imag, pupil_b)):
                kept[rows] = jnp.where(
                    left, pltpu.roll(value, low, 1), pltpu.roll(value, high, 1)
                )

    product = dot(table("wide_early", 0, th), partial)

    halo_copy.wait()
    product = product + dot(table("row_amb"), halo[...])
    sign = jnp.where(left, 1.0, -1.0)
    norm = 1.0 / math.sqrt((th + 2 * AMB) * tw)
    spec = norm * (product[:K] + sign * pltpu.roll(product[K:], K, 1))
    turned = -sign * pltpu.roll(spec, K, 1)

    fields = 3 * local
    masked = [
        pupil_a[q * K : (q + 1) * K] * spec + pupil_b[q * K : (q + 1) * K] * turned
        for q in range(fields)
    ]
    cols = dot(jnp.concatenate(masked, 0).astype(jnp.bfloat16), table("wide_early", th))
    cols = cols.astype(jnp.bfloat16)
    mixed = [
        jnp.concatenate([cols[q * K : (q + 1) * K, :grid], cols[q * K : (q + 1) * K, grid:]], 0)
        for q in range(fields)
    ]
    field[...] = dot(table("row_inv"), jnp.concatenate(mixed, 1))
    total = jnp.zeros((grid, grid), jnp.float32)
    for s in range(local):
        power_s = jnp.zeros((grid, grid), jnp.float32)
        for q in range(3 * s, 3 * s + 3):
            values = field[:, q * grid : (q + 1) * grid]
            power_s = power_s + values[:grid] * values[:grid] + values[grid:] * values[grid:]
        power[s] = power_s
        total = total + (weights[s] / parts_total) * power_s
    part[...] = total.astype(jnp.bfloat16)

    def block(index):
        return pl.ds(pl.multiple_of(index * block_rows, block_rows), block_rows)

    def guarded(condition, run):
        if owners == n:
            run()
        else:
            pl.when(condition)(run)

    scatter, gather = {}, {}
    for step in range(1, n):
        peer = lax.rem(me + step, n)
        to = peer if owners == n else jnp.minimum(peer, owners - 1)
        scatter[step] = pltpu.make_async_remote_copy(
            src_ref=part.at[block(to)], dst_ref=landed.at[step],
            send_sem=scatter_send.at[step], recv_sem=scatter_recv.at[step],
            device_id={"src": peer},
        )
        guarded(peer < owners, scatter[step].start)
    mine = me if owners == n else jnp.minimum(me, owners - 1)

    def reduce_own():
        acc = part[block(mine), :].astype(jnp.float32)
        for step in range(1, n):
            scatter[step].wait_recv()
            acc = acc + landed[step].astype(jnp.float32)
        reduced[...] = acc.astype(jnp.bfloat16)
        for step in range(1, n):
            gather[step].start()
        whole[block(mine), :] = reduced[...]

    for step in range(1, n):
        peer = lax.rem(me + step, n)
        gather[step] = pltpu.make_async_remote_copy(
            src_ref=reduced, dst_ref=whole.at[block(mine)],
            send_sem=gather_send.at[step], recv_sem=gather_recv.at[step],
            device_id={"src": peer},
        )
    projected = dot(table("target").astype(jnp.bfloat16), table("d_col_t")).astype(jnp.bfloat16)
    target_small[...] = dot(table("wide_late", 0, th), projected)

    guarded(me < owners, reduce_own)
    row_inv_t = table("wide_late", th + 2 * grid, th + 4 * grid)
    col_back = table("tall_late", 0, 4 * K)
    gram = table("wide_late", th, th + 2 * grid)
    for step in range(1, n):
        origin = lax.rem(me + n - step, n)
        guarded(origin < owners, gather[step].wait_recv)

    image = whole[...]
    twice = jnp.concatenate([image, image], 0)
    residual = dot(gram, twice) - target_small[...]
    doubled = jnp.concatenate([residual, residual], 0)

    scaled = [
        (doubled * field[:, q * grid : (q + 1) * grid]).astype(jnp.bfloat16) for q in range(fields)
    ]
    rows = dot(row_inv_t, jnp.concatenate(scaled, 1)).astype(jnp.bfloat16)
    mixed = [
        jnp.concatenate([rows[:K, q * grid : (q + 1) * grid], rows[K:, q * grid : (q + 1) * grid]], 1)
        for q in range(fields)
    ]
    both = dot(jnp.concatenate(mixed, 0), col_back)
    grad = jnp.zeros((K, LANES), jnp.float32)
    scale = 2.0 / (parts_total * K)
    for s in range(local):
        own_grad = jnp.zeros((K, LANES), jnp.float32)
        for q in range(3 * s, 3 * s + 3):
            rows_q = slice(q * K, (q + 1) * K)
            pair = both[rows_q]
            own_grad = own_grad + pupil_a[rows_q] * pair[:, :LANES] + pupil_b[rows_q] * pair[:, LANES:]
        grad = grad + (scale * weights[s]) * own_grad
    spec_send[...] = (norm * grad).astype(jnp.bfloat16)

    spread, rims = {}, []
    for step in range(1, n):
        peer = lax.rem(me + step, n)
        spread[step] = pltpu.make_async_remote_copy(
            src_ref=spec_send, dst_ref=spec_land.at[step],
            send_sem=spec_ssem.at[step], recv_sem=spec_rsem.at[step],
            device_id={"src": peer},
        )
        spread[step].start()
    for e in range(edges):
        rims.append(
            pltpu.make_async_remote_copy(
                src_ref=spec_send, dst_ref=edge_land.at[me],
                send_sem=edge_ssem.at[e], recv_sem=edge_rsem.at[me],
                device_id={"src": e + tile * (n - edges), "tile": other},
            )
        )
        rims[-1].start()
    for s in range(local):
        sums[s : s + 1, :] = jnp.sum(residual * power[s], 0, keepdims=True)
    sums_copy = pltpu.make_async_remote_copy(
        src_ref=sums, dst_ref=sums_land, send_sem=sums_sem.at[0], recv_sem=sums_sem.at[1],
        device_id={"tile": other},
    )
    sums_copy.start()

    lines = dot(table("own_rows", 0, 2 * grid), twice)
    lines_high = lines.astype(jnp.bfloat16)
    lines_low = (lines - lines_high.astype(jnp.float32)).astype(jnp.bfloat16)
    image_out[...] = dot(jnp.concatenate([lines_high, lines_low], 1), table("tall_late", 4 * K))

    writes = [
        pltpu.make_async_copy(source, to, out_sem.at[i])
        for i, (source, to) in enumerate(zip((image_out, grad_out, source_out), outputs))
    ]
    writes[0].start()

    row_back, amb_back = table("own_rows", 2 * grid), table("amb_back")
    col_fwd_t = table("wide_late", th + 4 * grid)
    sums_copy.wait()
    both_sums = jnp.sum(sums[...] + sums_land[...], 1, keepdims=True) / (2 * th * tw)
    for s in range(local):
        source_out[s] = both_sums[s, 0]
    writes[2].start()

    for step in range(1, n):
        guarded(lax.rem(me + step, n) < owners, scatter[step].wait_send)
        guarded(me < owners, gather[step].wait_send)

    def stack(value):
        return jnp.concatenate([value, -sign * pltpu.roll(value, K, 1)], 0).astype(jnp.bfloat16)

    summed = spec_send[...].astype(jnp.float32)
    for step in range(1, n):
        spread[step].wait_recv()
        summed = summed + spec_land[step].astype(jnp.float32)
    rows = dot(row_back, stack(summed))
    at_rim = jnp.where(tile == 0, me >= n - edges, me < edges)

    @pl.when(at_rim)
    def _():
        outer = jnp.zeros((K, LANES), jnp.float32)
        for d in range(n):
            pltpu.make_async_remote_copy(
                src_ref=spec_send, dst_ref=edge_land.at[d],
                send_sem=edge_ssem.at[0], recv_sem=edge_rsem.at[d],
                device_id={"tile": other},
            ).wait_recv()
            outer = outer + edge_land[d].astype(jnp.float32)
        full = rows + dot(amb_back, stack(outer))
        grad_out[...] = GRAD_SCALE * dot(full.astype(jnp.bfloat16), col_fwd_t)

    @pl.when(jnp.logical_not(at_rim))
    def _():
        grad_out[...] = GRAD_SCALE * dot(rows.astype(jnp.bfloat16), col_fwd_t)

    writes[1].start()
    for step in range(1, n):
        spread[step].wait_send()
    for copy in rims:
        copy.wait_send()
    for copy in writes:
        copy.wait()


def write_outputs(image, grad, source, image_out, grad_out, source_out, held, scalars, sem):
    ways = [
        (image, held.at[0], image_out.at[0]),
        (grad, held.at[1], grad_out.at[0]),
        (source, scalars, source_out),
    ]
    loads = [pltpu.make_async_copy(w[0], w[1], sem.at[0, i]) for i, w in enumerate(ways)]
    stores = [pltpu.make_async_copy(w[1], w[2], sem.at[1, i]) for i, w in enumerate(ways)]
    for load in loads:
        load.start()
    for load, store in zip(loads, stores):
        load.wait()
        store.start()
    for store in stores:
        store.wait()


def body(
    mask_values, target_image, jones_pupil, polar_states, source_weights, pupil_offsets, polar_ids
):
    th, tw = mask_values.shape
    n = lax.axis_size("src")
    assert lax.axis_size("tile") == 2
    local = source_weights.shape[0]
    share = th // n
    grid = 2 * K
    owners = min(n, grid // ROWS_16)
    block_rows = grid // owners
    assert owners * block_rows == grid
    edges = -(-AMB // share)
    named = dict(
        mask=mask_values,
        target=target_image,
        jones=jones_pupil.reshape((-1,) + jones_pupil.shape[-2:]),
        offsets=pupil_offsets.T,
        ids=polar_ids,
        weights=source_weights,
        polar=polar_states.transpose(1, 2, 0),
    )
    constants = tables(th, tw)
    order = ["mask", "col_fwd", *SCALARS, "jones", "wide_early", "row_amb", "row_inv", "target"]
    order += [name for name in constants if name not in order]
    arrays = []
    held = []
    for name in order:
        value = named[name] if name in named else jnp.asarray(constants[name])
        arrays.append(value)
        shape = value.shape
        if name == "amb_back":
            shape = (share,) + shape[2:]
        elif name == "row_amb":
            shape = shape[1:]
        elif name == "own_rows":
            shape = (share,) + shape[1:]
        held.append((pltpu.SMEM if name in SCALARS else pltpu.VMEM)(shape, value.dtype))
    f32, bf16 = jnp.float32, jnp.bfloat16
    sems = pltpu.SemaphoreType.DMA
    scratch = held + [
        pltpu.VMEM((AMB, tw), bf16),
        pltpu.VMEM((AMB, LANES), bf16),
        pltpu.VMEM((AMB, LANES), bf16),
        pltpu.VMEM((3 * local * K, LANES), f32),
        pltpu.VMEM((3 * local * K, LANES), f32),
        pltpu.VMEM((2 * grid, 3 * local * grid), f32),
        pltpu.VMEM((local, grid, grid), f32),
        pltpu.VMEM((grid, grid), f32),
        pltpu.VMEM((grid, grid), bf16),
        pltpu.VMEM((n, block_rows, grid), bf16),
        pltpu.VMEM((block_rows, grid), bf16),
        pltpu.VMEM((grid, grid), bf16),
        pltpu.VMEM((K, LANES), bf16),
        pltpu.VMEM((n, K, LANES), bf16),
        pltpu.VMEM((n, K, LANES), bf16),
        pltpu.VMEM((local, LANES), f32),
        pltpu.VMEM((local, LANES), f32),
        sems((len(order) + 1,)),
        sems((2,)),
        sems((n,)),
        sems((n,)),
        sems((n,)),
        sems((n,)),
        sems((n,)),
        sems((n,)),
        sems((edges,)),
        sems((n,)),
        sems((2,)),
        pltpu.VMEM((share, tw), f32),
        pltpu.VMEM((share, tw), f32),
        pltpu.SMEM((local,), f32),
        sems((3,)),
    ]
    sizes = (n, local, th, tw, share, owners, block_rows, edges, local * n)
    in_hbm = pl.BlockSpec(memory_space=pltpu.HBM)
    results = pl.pallas_call(
        functools.partial(kernel, tuple(order), sizes),
        out_shape=(
            jax.ShapeDtypeStruct((share, tw), f32),
            jax.ShapeDtypeStruct((share, tw), f32),
            jax.ShapeDtypeStruct((local,), f32),
        ),
        in_specs=[in_hbm] * len(arrays),
        out_specs=(in_hbm,) * 3,
        scratch_shapes=scratch,
        compiler_params=pltpu.CompilerParams(
            collective_id=0, has_side_effects=True, vmem_limit_bytes=VMEM_LIMIT
        ),
    )(*arrays)
    return pl.pallas_call(
        write_outputs,
        out_shape=(
            jax.ShapeDtypeStruct((1, share, tw), f32),
            jax.ShapeDtypeStruct((1, share, tw), f32),
            jax.ShapeDtypeStruct((local,), f32),
        ),
        in_specs=[in_hbm] * 3,
        out_specs=(in_hbm,) * 3,
        scratch_shapes=[pltpu.VMEM((2, share, tw), f32), pltpu.SMEM((local,), f32), sems((2, 3))],
        compiler_params=pltpu.CompilerParams(vmem_limit_bytes=VMEM_LIMIT),
    )(*results)


def solution(mesh):
    placed = (
        P(("parts", "tile"), None),
        P(("parts", "tile"), None),
        P(),
        P(),
        P(("parts", "src")),
        P(("parts", "src"), None),
        P(("parts", "src")),
    )
    return jax.shard_map(
        body,
        mesh=mesh,
        in_specs=placed,
        out_specs=(
            P(("parts", "tile"), "src", None),
            P(("parts", "tile"), "src", None),
            P(("parts", "src")),
        ),
        check_vma=False,
    )
```

```python
import functools
import math

import jax
import jax.numpy as jnp
import ml_dtypes
import numpy as np
from jax import lax
from jax.experimental import pallas as pl
from jax.experimental.pallas import tpu as pltpu
from jax.sharding import PartitionSpec as P

AMB = 64
K = 64
GRAD_SCALE = 32.0
LANES = 2 * K
VMEM_LIMIT = 64 * 1024 * 1024 - 512 * 1024
ROWS_16 = 16


def split_bf16(table):
    high = table.astype(ml_dtypes.bfloat16)
    low = (table - high.astype(np.float64)).astype(ml_dtypes.bfloat16)
    return high, low


def tables(th, tw):
    window = th + 2 * AMB
    grid = 2 * K
    orders = np.arange(K) - K // 2
    diffs = np.arange(-(K - 1), K)

    def angle(left, right, period):
        return 2.0 * np.pi * np.mod(np.outer(left, right), period) / period

    bf = lambda x: np.ascontiguousarray(x).astype(ml_dtypes.bfloat16)
    col = angle(np.arange(tw), orders, tw)
    col_fwd = np.concatenate([np.cos(col), -np.sin(col)], 1)
    row = angle(orders, np.arange(window), window)
    row_fwd = np.concatenate([np.cos(row), np.sin(row)], 0)
    row_amb = np.stack([row_fwd[:, th + AMB :], row_fwd[:, :AMB]])
    row_back = row_fwd[:, AMB : AMB + th].T
    amb_back = np.zeros((2, th, 2 * K))
    amb_back[0, th - AMB :] = row_fwd[:, :AMB].T
    amb_back[1, :AMB] = row_fwd[:, th + AMB :].T
    small = angle(np.arange(grid), orders, grid)
    cos, sin = np.cos(small), np.sin(small)
    row_inv = np.concatenate(
        [np.concatenate([cos, -sin], 1), np.concatenate([sin, cos], 1)], 0
    )
    col_inv = np.concatenate(
        [np.concatenate([cos.T, sin.T], 1), np.concatenate([-sin.T, cos.T], 1)], 0
    )
    back = col_inv.T
    col_back = np.concatenate([back, back[:, K:], -back[:, :K]], 1)

    def dirichlet(positions):
        turn = positions[:, None] - np.arange(grid)[None, :] / grid
        return np.cos(2.0 * np.pi * turn[:, :, None] * diffs).sum(-1) / grid

    d_row = dirichlet((np.arange(th) + AMB) / window)
    d_col = dirichlet(np.arange(tw) / tw)
    gram = (tw / grid) * (d_row.T @ d_row)
    cat = lambda *parts: np.concatenate(parts, 1)
    wide_early = cat(bf(row_fwd[:, AMB : AMB + th]), bf(col_inv / K))
    wide_late = cat(bf(d_row.T), *split_bf16(gram), bf(row_inv.T), bf(col_fwd.T))
    tall_late = cat(bf(col_back), bf(np.concatenate([d_col.T, d_col.T], 0)))
    own_rows = cat(*split_bf16(d_row), bf(row_back))
    return dict(
        col_fwd=bf(col_fwd),
        wide_early=wide_early,
        row_amb=bf(row_amb),
        row_inv=bf(row_inv),
        d_col_t=bf(d_col),
        wide_late=wide_late,
        tall_late=tall_late,
        own_rows=own_rows,
        amb_back=bf(amb_back),
    )


SCALARS = ("offsets", "ids", "weights", "polar")
FIRST = ("rim", "col_fwd", "mask")


def dot(a, b):
    return jnp.dot(a, b, preferred_element_type=jnp.float32)


def kernel(names, sizes, *refs):
    n, local, th, tw, share, owners, block_rows, edges, parts_total = sizes
    grid = 2 * K
    count = len(names)
    hbm = dict(zip(names, refs[:count]))
    outputs = refs[count : 3 + count]
    vmem = dict(zip(names, refs[3 + count : 3 + 2 * count]))
    offsets, ids, weights, polar = (vmem[name] for name in SCALARS)
    (
        rim_rows, rim_send, halo, pupil_a, pupil_b, field, power, target_small,
        part, landed, reduced, whole, spec_send, spec_land, edge_land, sums, sums_land,
        load_sem, halo_sem, scatter_send, scatter_recv, gather_send, gather_recv,
        spec_ssem, spec_rsem, edge_ssem, edge_rsem, sums_sem,
        image_out, grad_out, source_out, out_sem,
    ) = refs[3 + 2 * count :]
    me = lax.axis_index("src")
    tile = lax.axis_index("tile")
    other = 1 - tile

    own = pl.ds(pl.multiple_of(me * share, share), share)
    rim = pl.ds(pl.multiple_of(other * (th - AMB), ROWS_16), AMB)
    parts_of = {
        "rim": lambda ref: ref.at[rim],
        "amb_back": lambda ref: ref.at[tile, own],
        "row_amb": lambda ref: ref.at[tile],
        "own_rows": lambda ref: ref.at[own],
    }
    loads = {}

    def load(chosen):
        for name in chosen:
            source = hbm["mask" if name == "rim" else name]
            source = parts_of[name](source) if name in parts_of else source
            target = rim_rows if name == "rim" else vmem[name]
            loads[name] = pltpu.make_async_copy(source, target, load_sem.at[len(loads)])
            loads[name].start()

    load(FIRST)
    barrier = pltpu.get_barrier_semaphore()
    for step in range(n):
        peer = lax.rem(me + step, n)
        if step:
            pl.semaphore_signal(barrier, inc=1, device_id={"src": peer, "tile": tile})
        pl.semaphore_signal(barrier, inc=1, device_id={"src": peer, "tile": other})
    load([name for name in names if name not in FIRST])
    waited = set()

    def table(name, start=0, stop=None):
        if name not in waited:
            loads[name].wait()
            waited.add(name)
        return vmem[name][:, start:stop]

    loads["rim"].wait()
    rim_send[...] = dot(rim_rows[...], table("col_fwd")).astype(jnp.bfloat16)
    pl.semaphore_wait(barrier, 2 * n - 1)
    halo_copy = pltpu.make_async_remote_copy(
        src_ref=rim_send, dst_ref=halo, send_sem=halo_sem.at[0], recv_sem=halo_sem.at[1],
        device_id={"tile": other},
    )
    halo_copy.start()
    partial = dot(table("mask"), table("col_fwd")).astype(jnp.bfloat16)

    for name in SCALARS + ("jones",):
        loads[name].wait()
    jones = vmem["jones"]
    lane = lax.broadcasted_iota(jnp.int32, (K, LANES), 1)
    left = lane < K
    for s in range(local):
        first, second, state = offsets[0, s], offsets[1, s], ids[s]
        low = lax.rem(LANES - second, LANES)
        high = K - second
        vec = [[polar[c, i, state] for i in range(2)] for c in range(2)]
        for j in range(3):
            win = [
                [jones[(c * 3 + j) * 2 + i, pl.ds(first, K), :] for i in range(2)]
                for c in range(2)
            ]
            real = sum(win[0][i] * vec[0][i] - win[1][i] * vec[1][i] for i in range(2))
            imag = sum(win[0][i] * vec[1][i] + win[1][i] * vec[0][i] for i in range(2))
            rows = slice((s * 3 + j) * K, (s * 3 + j + 1) * K)
            for value, kept in ((real, pupil_a), (imag, pupil_b)):
                kept[rows] = jnp.where(
                    left, pltpu.roll(value, low, 1), pltpu.roll(value, high, 1)
                )

    product = dot(table("wide_early", 0, th), partial)

    halo_copy.wait()
    product = product + dot(table("row_amb"), halo[...])
    sign = jnp.where(left, 1.0, -1.0)
    norm = 1.0 / math.sqrt((th + 2 * AMB) * tw)
    spec = norm * (product[:K] + sign * pltpu.roll(product[K:], K, 1))
    turned = -sign * pltpu.roll(spec, K, 1)

    fields = 3 * local
    masked = [
        pupil_a[q * K : (q + 1) * K] * spec + pupil_b[q * K : (q + 1) * K] * turned
        for q in range(fields)
    ]
    cols = dot(jnp.concatenate(masked, 0).astype(jnp.bfloat16), table("wide_early", th))
    cols = cols.astype(jnp.bfloat16)
    mixed = [
        jnp.concatenate([cols[q * K : (q + 1) * K, :grid], cols[q * K : (q + 1) * K, grid:]], 0)
        for q in range(fields)
    ]
    field[...] = dot(table("row_inv"), jnp.concatenate(mixed, 1))
    total = jnp.zeros((grid, grid), jnp.float32)
    for s in range(local):
        power_s = jnp.zeros((grid, grid), jnp.float32)
        for q in range(3 * s, 3 * s + 3):
            values = field[:, q * grid : (q + 1) * grid]
            power_s = power_s + values[:grid] * values[:grid] + values[grid:] * values[grid:]
        power[s] = power_s
        total = total + (weights[s] / parts_total) * power_s
    part[...] = total.astype(jnp.bfloat16)

    def block(index):
        return pl.ds(pl.multiple_of(index * block_rows, block_rows), block_rows)

    def wait_all(slots, sem):
        taken = slots.at[pl.ds(1, n - 1)]
        pltpu.make_async_copy(taken, taken, sem.at[0]).wait()

    def guarded(condition, run):
        if owners == n:
            run()
        else:
            pl.when(condition)(run)

    scatter, gather = {}, {}
    for step in range(1, n):
        peer = lax.rem(me + step, n)
        to = peer if owners == n else jnp.minimum(peer, owners - 1)
        scatter[step] = pltpu.make_async_remote_copy(
            src_ref=part.at[block(to)], dst_ref=landed.at[step],
            send_sem=scatter_send.at[step], recv_sem=scatter_recv.at[0],
            device_id={"src": peer},
        )
        guarded(peer < owners, scatter[step].start)
    mine = me if owners == n else jnp.minimum(me, owners - 1)

    def reduce_own():
        acc = part[block(mine), :].astype(jnp.float32)
        wait_all(landed, scatter_recv)
        for step in range(1, n):
            acc = acc + landed[step].astype(jnp.float32)
        reduced[...] = acc.astype(jnp.bfloat16)
        for step in range(1, n):
            gather[step].start()
        whole[block(mine), :] = reduced[...]

    for step in range(1, n):
        peer = lax.rem(me + step, n)
        gather[step] = pltpu.make_async_remote_copy(
            src_ref=reduced, dst_ref=whole.at[block(mine)],
            send_sem=gather_send.at[step], recv_sem=gather_recv.at[step],
            device_id={"src": peer},
        )
    projected = dot(table("target").astype(jnp.bfloat16), table("d_col_t")).astype(jnp.bfloat16)
    target_small[...] = dot(table("wide_late", 0, th), projected)

    guarded(me < owners, reduce_own)
    row_inv_t = table("wide_late", th + 2 * grid, th + 4 * grid)
    col_back = table("tall_late", 0, 4 * K)
    gram = table("wide_late", th, th + 2 * grid)
    for step in range(1, n):
        origin = lax.rem(me + n - step, n)
        guarded(origin < owners, gather[step].wait_recv)

    image = whole[...]
    twice = jnp.concatenate([image, image], 0)
    residual = dot(gram, twice) - target_small[...]
    doubled = jnp.concatenate([residual, residual], 0)

    scaled = [
        (doubled * field[:, q * grid : (q + 1) * grid]).astype(jnp.bfloat16) for q in range(fields)
    ]
    rows = dot(row_inv_t, jnp.concatenate(scaled, 1)).astype(jnp.bfloat16)
    mixed = [
        jnp.concatenate([rows[:K, q * grid : (q + 1) * grid], rows[K:, q * grid : (q + 1) * grid]], 1)
        for q in range(fields)
    ]
    both = dot(jnp.concatenate(mixed, 0), col_back)
    grad = jnp.zeros((K, LANES), jnp.float32)
    scale = 2.0 / (parts_total * K)
    for s in range(local):
        own_grad = jnp.zeros((K, LANES), jnp.float32)
        for q in range(3 * s, 3 * s + 3):
            rows_q = slice(q * K, (q + 1) * K)
            pair = both[rows_q]
            own_grad = own_grad + pupil_a[rows_q] * pair[:, :LANES] + pupil_b[rows_q] * pair[:, LANES:]
        grad = grad + (scale * weights[s]) * own_grad
    spec_send[...] = (norm * grad).astype(jnp.bfloat16)

    spread, rims = {}, []
    for step in range(1, n):
        peer = lax.rem(me + step, n)
        spread[step] = pltpu.make_async_remote_copy(
            src_ref=spec_send, dst_ref=spec_land.at[step],
            send_sem=spec_ssem.at[step], recv_sem=spec_rsem.at[0],
            device_id={"src": peer},
        )
        spread[step].start()
    for e in range(edges):
        rims.append(
            pltpu.make_async_remote_copy(
                src_ref=spec_send, dst_ref=edge_land.at[me],
                send_sem=edge_ssem.at[e], recv_sem=edge_rsem.at[me],
                device_id={"src": e + tile * (n - edges), "tile": other},
            )
        )
        rims[-1].start()
    for s in range(local):
        sums[s : s + 1, :] = jnp.sum(residual * power[s], 0, keepdims=True)
    sums_copy = pltpu.make_async_remote_copy(
        src_ref=sums, dst_ref=sums_land, send_sem=sums_sem.at[0], recv_sem=sums_sem.at[1],
        device_id={"tile": other},
    )
    sums_copy.start()

    lines = dot(table("own_rows", 0, 2 * grid), twice)
    lines_high = lines.astype(jnp.bfloat16)
    lines_low = (lines - lines_high.astype(jnp.float32)).astype(jnp.bfloat16)
    image_out[...] = dot(jnp.concatenate([lines_high, lines_low], 1), table("tall_late", 4 * K))

    writes = [
        pltpu.make_async_copy(source, to, out_sem.at[i])
        for i, (source, to) in enumerate(zip((image_out, grad_out, source_out), outputs))
    ]
    writes[0].start()

    row_back, amb_back = table("own_rows", 2 * grid), table("amb_back")
    col_fwd_t = table("wide_late", th + 4 * grid)
    sums_copy.wait()
    both_sums = jnp.sum(sums[...] + sums_land[...], 1, keepdims=True) / (2 * th * tw)
    for s in range(local):
        source_out[s] = both_sums[s, 0]
    writes[2].start()

    def stack(value):
        return jnp.concatenate([value, -sign * pltpu.roll(value, K, 1)], 0).astype(jnp.bfloat16)

    summed = spec_send[...].astype(jnp.float32)
    wait_all(spec_land, spec_rsem)
    for step in range(1, n):
        summed = summed + spec_land[step].astype(jnp.float32)
    rows = dot(row_back, stack(summed))
    at_rim = jnp.where(tile == 0, me >= n - edges, me < edges)

    @pl.when(at_rim)
    def _():
        outer = jnp.zeros((K, LANES), jnp.float32)
        for d in range(n):
            pltpu.make_async_remote_copy(
                src_ref=spec_send, dst_ref=edge_land.at[d],
                send_sem=edge_ssem.at[0], recv_sem=edge_rsem.at[d],
                device_id={"tile": other},
            ).wait_recv()
            outer = outer + edge_land[d].astype(jnp.float32)
        full = rows + dot(amb_back, stack(outer))
        grad_out[...] = GRAD_SCALE * dot(full.astype(jnp.bfloat16), col_fwd_t)

    @pl.when(jnp.logical_not(at_rim))
    def _():
        grad_out[...] = GRAD_SCALE * dot(rows.astype(jnp.bfloat16), col_fwd_t)

    writes[1].start()
    for step in range(1, n):
        guarded(lax.rem(me + step, n) < owners, scatter[step].wait_send)
        guarded(me < owners, gather[step].wait_send)
        spread[step].wait_send()
    for copy in rims:
        copy.wait_send()
    for copy in writes:
        copy.wait()


def write_outputs(image, grad, source, image_out, grad_out, source_out, held, scalars, sem):
    ways = [
        (image, held.at[0], image_out.at[0]),
        (grad, held.at[1], grad_out.at[0]),
        (source, scalars, source_out),
    ]
    loads = [pltpu.make_async_copy(w[0], w[1], sem.at[0, i]) for i, w in enumerate(ways)]
    stores = [pltpu.make_async_copy(w[1], w[2], sem.at[1, i]) for i, w in enumerate(ways)]
    for load in loads:
        load.start()
    for load, store in zip(loads, stores):
        load.wait()
        store.start()
    for store in stores:
        store.wait()


def body(
    mask_values, target_image, jones_pupil, polar_states, source_weights, pupil_offsets, polar_ids
):
    th, tw = mask_values.shape
    n = lax.axis_size("src")
    assert lax.axis_size("tile") == 2
    local = source_weights.shape[0]
    share = th // n
    grid = 2 * K
    owners = min(n, grid // ROWS_16)
    block_rows = grid // owners
    assert owners * block_rows == grid
    edges = -(-AMB // share)
    named = dict(
        mask=mask_values,
        target=target_image,
        jones=jones_pupil.reshape((-1,) + jones_pupil.shape[-2:]),
        offsets=pupil_offsets.T,
        ids=polar_ids,
        weights=source_weights,
        polar=polar_states.transpose(1, 2, 0),
    )
    constants = tables(th, tw)
    order = ["mask", "col_fwd", *SCALARS, "jones", "wide_early", "row_amb", "row_inv", "target"]
    order += [name for name in constants if name not in order]
    arrays = []
    held = []
    for name in order:
        value = named[name] if name in named else jnp.asarray(constants[name])
        arrays.append(value)
        shape = value.shape
        if name == "amb_back":
            shape = (share,) + shape[2:]
        elif name == "row_amb":
            shape = shape[1:]
        elif name == "own_rows":
            shape = (share,) + shape[1:]
        held.append((pltpu.SMEM if name in SCALARS else pltpu.VMEM)(shape, value.dtype))
    f32, bf16 = jnp.float32, jnp.bfloat16
    sems = pltpu.SemaphoreType.DMA
    scratch = held + [
        pltpu.VMEM((AMB, tw), bf16),
        pltpu.VMEM((AMB, LANES), bf16),
        pltpu.VMEM((AMB, LANES), bf16),
        pltpu.VMEM((3 * local * K, LANES), f32),
        pltpu.VMEM((3 * local * K, LANES), f32),
        pltpu.VMEM((2 * grid, 3 * local * grid), f32),
        pltpu.VMEM((local, grid, grid), f32),
        pltpu.VMEM((grid, grid), f32),
        pltpu.VMEM((grid, grid), bf16),
        pltpu.VMEM((n, block_rows, grid), bf16),
        pltpu.VMEM((block_rows, grid), bf16),
        pltpu.VMEM((grid, grid), bf16),
        pltpu.VMEM((K, LANES), bf16),
        pltpu.VMEM((n, K, LANES), bf16),
        pltpu.VMEM((n, K, LANES), bf16),
        pltpu.VMEM((local, LANES), f32),
        pltpu.VMEM((local, LANES), f32),
        sems((len(order) + 1,)),
        sems((2,)),
        sems((n,)),
        sems((n,)),
        sems((n,)),
        sems((n,)),
        sems((n,)),
        sems((n,)),
        sems((edges,)),
        sems((n,)),
        sems((2,)),
        pltpu.VMEM((share, tw), f32),
        pltpu.VMEM((share, tw), f32),
        pltpu.SMEM((local,), f32),
        sems((3,)),
    ]
    sizes = (n, local, th, tw, share, owners, block_rows, edges, local * n)
    in_hbm = pl.BlockSpec(memory_space=pltpu.HBM)
    results = pl.pallas_call(
        functools.partial(kernel, tuple(order), sizes),
        out_shape=(
            jax.ShapeDtypeStruct((share, tw), f32),
            jax.ShapeDtypeStruct((share, tw), f32),
            jax.ShapeDtypeStruct((local,), f32),
        ),
        in_specs=[in_hbm] * len(arrays),
        out_specs=(in_hbm,) * 3,
        scratch_shapes=scratch,
        compiler_params=pltpu.CompilerParams(
            collective_id=0, has_side_effects=True, vmem_limit_bytes=VMEM_LIMIT
        ),
    )(*arrays)
    return pl.pallas_call(
        write_outputs,
        out_shape=(
            jax.ShapeDtypeStruct((1, share, tw), f32),
            jax.ShapeDtypeStruct((1, share, tw), f32),
            jax.ShapeDtypeStruct((local,), f32),
        ),
        in_specs=[in_hbm] * 3,
        out_specs=(in_hbm,) * 3,
        scratch_shapes=[pltpu.VMEM((2, share, tw), f32), pltpu.SMEM((local,), f32), sems((2, 3))],
        compiler_params=pltpu.CompilerParams(vmem_limit_bytes=VMEM_LIMIT),
    )(*results)


def solution(mesh):
    placed = (
        P(("parts", "tile"), None),
        P(("parts", "tile"), None),
        P(),
        P(),
        P(("parts", "src")),
        P(("parts", "src"), None),
        P(("parts", "src")),
    )
    return jax.shard_map(
        body,
        mesh=mesh,
        in_specs=placed,
        out_specs=(
            P(("parts", "tile"), "src", None),
            P(("parts", "tile"), "src", None),
            P(("parts", "src")),
        ),
        check_vma=False,
    )
```
